128 devices in a mesh: dom: 16 (over z, y_lo, core), loop: 8 (over y_hi, x).
Axes of the slice: x: 4, y: 4 (y_hi: 2, y_lo: 2; y = y_hi * 2 + y_lo), z: 4, core: 2. Of those that a mesh axis runs over, the one named last changes fastest.
Arguments:
- cotangent: bfloat16 [131072, 256], P(('dom', 'loop')), may hold values from -6 to 6
- preact: bfloat16 [131072, 256], P(('dom', 'loop')), may hold values from -6 to 6
- aggregated: bfloat16 [131072, 256], P(('dom', 'loop')), may hold values from -6 to 6
- weight: bfloat16 [256, 256], replicated, may hold values from -0.375 to 0.375
- tile_values: bfloat16 [81920, 128, 128], P(('dom', 'loop')), as said below
- tile_rows: int32 [128, 640], P(('dom', 'loop')), may hold values from 0 to 63
- tile_cols: int32 [128, 640], P(('dom', 'loop')), may hold values from 0 to 127, as said below
- tile_counts: int32 [128], P(('dom', 'loop')), may hold values from 64 to 640
Outputs:
- node_grad: float32 [131072, 256], P(('dom', 'loop'))
- weight_grad: float32 [256, 256], replicated
The draws below stay inside these ranges and needn't reach their ends.
Inputs may be any that keep to these rules, and one draw needn't show every extreme that they name: `tile_cols`: the live tiles of one device touch, for every dom index, exactly 4 distinct column blocks, and every tile's column lies among them. `tile_values`: entries are nonnegative.
All inputs are finite; a program needn't handle non-finite values.
Results may differ from the reference program's by a relative error of at most 0.0029.
Values may be sent and summed in bfloat16 or wider, within the bound.
A program may use at most 192 MiB of HBM per device.

```python
import math
import jax
import jax.numpy as jnp
from jax import lax

F = 256
TILE = 128
RB_DEV = 8
CAP = 4
TILES_DEV = 640
NODES = 131072
N_DOM = 16
N_LOOP = 8
DEVICES = 128


def draw_tile_values(key, part):
    scale = (TILE * TILES_DEV // RB_DEV) ** (-0.5)
    shape = (DEVICES * TILES_DEV, TILE, TILE)
    values = jnp.minimum(jnp.abs(jax.random.normal(jax.random.fold_in(key, 32), shape, jnp.float32)), 6.0) * scale
    return values.astype(jnp.bfloat16)


def draw_tile_cols(key, part):
    keys = jax.random.split(jax.random.fold_in(key, 11), DEVICES * N_DOM)
    orders = jax.vmap(lambda single: jax.random.permutation(single, RB_DEV))(keys).reshape(DEVICES, N_DOM, RB_DEV)
    chosen = orders[:, :, :CAP]
    allowed = (jnp.arange(N_DOM, dtype=jnp.int32)[None, :, None] * RB_DEV + chosen).reshape(DEVICES, N_DOM * CAP)
    keys_two = jax.random.split(jax.random.fold_in(key, 12), DEVICES)
    spread = jax.vmap(lambda single: jax.random.permutation(single, N_DOM * CAP))(keys_two)
    first = jnp.take_along_axis(allowed, spread, axis=1)
    extra = jax.random.randint(jax.random.fold_in(key, 13), (DEVICES, TILES_DEV - N_DOM * CAP), 0, N_DOM * CAP)
    second = jnp.take_along_axis(allowed, extra, axis=1)
    return jnp.concatenate([first, second], axis=1).astype(jnp.int32)


def draw_tile_counts(key, part):
    lowest = N_DOM * CAP
    span = TILES_DEV - lowest
    first = jax.random.randint(jax.random.fold_in(key, 21), (DEVICES,), 0, span + 1)
    second = jax.random.randint(jax.random.fold_in(key, 22), (DEVICES,), 0, span + 1)
    counts = lowest + first * second // max(span, 1)
    fullest = jax.random.randint(jax.random.fold_in(key, 23), (), 0, DEVICES)
    return counts.at[fullest].set(TILES_DEV).astype(jnp.int32)


def with_ends(array, key, least, largest):
    place = [jax.random.randint(jax.random.fold_in(key, axis), (), 0, length) for axis, length in enumerate(array.shape)]
    longest = array.shape.index(max(array.shape))
    beside = place[:longest] + [(place[longest] + 1) % array.shape[longest]] + place[longest + 1:]
    return array.at[tuple(place)].set(least).at[tuple(beside)].set(largest)


def levels(key, dims, cuts, smallest, largest):
    gain = 1.0
    for position, parts in cuts:
        steps = jax.random.uniform(jax.random.fold_in(jax.random.fold_in(key, 6), position), (parts,), jnp.float32, smallest / len(cuts), largest / len(cuts))
        gain = gain * jnp.repeat(jnp.exp(steps), dims[position] // parts).reshape((-1,) + (1,) * (len(dims) - 1 - position))
    return gain


def gaussian(stream_key, extent, scale, limit, cuts=(), held_as=jnp.bfloat16):
    entries = scale * jax.random.normal(stream_key, extent, jnp.float32)
    if cuts:
        entries = entries * levels(stream_key, extent, cuts, -0.22, 0.18)
    return jnp.clip(entries, -limit, limit).astype(held_as)


def setup_inputs(seed: int = 0) -> dict:
    key_list = jax.random.split(jax.random.key(seed), 9)
    return {
        "cotangent": gaussian(key_list[0], (NODES, F), 1.0, 6.0, ((0, 128),)),
        "preact": gaussian(key_list[1], (NODES, F), 1.0, 6.0, ((0, 128),)),
        "aggregated": gaussian(key_list[2], (NODES, F), 1.0, 6.0, ((0, 128),)),
        "weight": gaussian(key_list[3], (F, F), F ** -0.5, 0.375),
        "tile_values": draw_tile_values(jax.random.fold_in(key_list[8], 71), 0),
        "tile_rows": with_ends(jax.random.randint(key_list[5], (DEVICES, TILES_DEV), 0, N_LOOP * RB_DEV), jax.random.fold_in(key_list[5], 1), 0, (N_LOOP * RB_DEV) - 1).astype(jnp.int32),
        "tile_cols": draw_tile_cols(jax.random.fold_in(key_list[8], 71), 0),
        "tile_counts": draw_tile_counts(jax.random.fold_in(key_list[8], 71), 0),
    }


def reference(cotangent, preact, aggregated, weight, tile_values, tile_rows, tile_cols, tile_counts):
    masked = jnp.where(preact > 0, cotangent, jnp.zeros_like(cotangent))
    weight_grad = jnp.dot(aggregated.T, masked, preferred_element_type=jnp.float32) * (1.0 / math.sqrt(NODES))
    projected = jnp.dot(masked, weight.T, preferred_element_type=jnp.float32).astype(jnp.bfloat16)
    row_blocks = projected.reshape(NODES // TILE, TILE, F)
    part_blocks = N_LOOP * RB_DEV
    values = tile_values.reshape(DEVICES, TILES_DEV, TILE, TILE)

    def one_device(totals, item):
        index, tile_vals, rows_here, cols_here, count = item
        dom_index = index // N_LOOP
        loop_index = index % N_LOOP
        source = (dom_index * part_blocks + rows_here).astype(jnp.int32)
        target = (cols_here // RB_DEV * part_blocks + loop_index * RB_DEV + cols_here % RB_DEV).astype(jnp.int32)
        picked = row_blocks[source].astype(jnp.float32)
        terms = jnp.einsum('tij,tif->tjf', tile_vals.astype(jnp.float32), picked, precision=lax.Precision.HIGHEST)
        alive = (jnp.arange(TILES_DEV, dtype=jnp.int32) < count).astype(jnp.float32)
        return (totals.at[target].add(terms * alive[:, None, None]), None)
    start = jnp.zeros((NODES // TILE, TILE, F), jnp.float32)
    totals = lax.scan(one_device, start, (jnp.arange(DEVICES, dtype=jnp.int32), values, tile_rows, tile_cols, tile_counts))[0]
    return (totals.reshape(NODES, F), weight_grad)
```

```python
import functools
import math

import jax
import jax.numpy as jnp
from jax import lax
from jax.experimental import pallas as pl
from jax.experimental.pallas import tpu as pltpu
from jax.sharding import PartitionSpec as P

MESH = pl.DeviceIdType.MESH
VMEM = pl.BlockSpec(memory_space=pltpu.VMEM)
ANY = pl.BlockSpec(memory_space=pl.ANY)
F32 = jnp.float32
BF16 = jnp.bfloat16

ROWS = 1024
F = 256
TILE = 128
BLOCKS = 8
X = 4
LOOP = 8
Z = 4
CHUNKS = 4
GROUP = 64


def remote(src, dst, send, recv, where):
    return pltpu.make_async_remote_copy(
        src_ref=src, dst_ref=dst, send_sem=send, recv_sem=recv, device_id=where, device_id_type=MESH
    )


def greet(peers):
    barrier = pltpu.get_barrier_semaphore()
    for peer in peers:
        pl.semaphore_signal(barrier, inc=1, device_id=peer, device_id_type=MESH)
    return barrier, len(peers)


def gather_kernel(cot, pre, agg, w, out, wpart, masked, send, recv):
    me = lax.axis_index("loop")
    x, h = lax.rem(me, X), me // X
    right = {"loop": h * X + lax.rem(x + 1, X)}
    left = {"loop": h * X + lax.rem(x + X - 1, X)}
    across = {"loop": (1 - h) * X + x}
    barrier, arrivals = greet([right, left, across])

    size = ROWS // CHUNKS
    half = CHUNKS // 2

    def piece(high, step, c):
        return out.at[high * X + lax.rem(x + step, X), pl.ds(c * size, size)]

    def copy(kind, c, ref, where):
        return remote(ref, ref, send.at[kind, c], recv.at[kind, c], where)

    for c in range(CHUNKS):
        rows = pl.ds(c * size, size)
        live = jnp.where(pre[rows].astype(F32) > 0, cot[rows].astype(F32), 0.0).astype(BF16)
        masked[rows] = live
        out[me, rows] = lax.dot_general(
            live, w[...], (((1,), (1,)), ((), ())), preferred_element_type=F32
        ).astype(BF16)
    pl.semaphore_wait(barrier, arrivals)
    sent = []

    def go(kind, c, ref, where):
        op = copy(kind, c, ref, where)
        op.start()
        sent.append(op)

    def arrive(kind, c, ref):
        copy(kind, c, ref, right).wait_recv()

    back = [CHUNKS - 1 - c for c in range(CHUNKS)]
    for c in range(CHUNKS):
        go(0, c, piece(h, 0, c), right)
        go(1, back[c], piece(h, 0, back[c]), left)
        go(2, c, piece(h, 0, c), across)

    total = jnp.zeros((F, F), F32)
    for c in range(CHUNKS):
        rows = pl.ds(c * size, size)
        total += lax.dot_general(
            agg[rows], masked[rows], (((0,), (0,)), ((), ())), preferred_element_type=F32
        )
    wpart[...] = total

    for c in range(CHUNKS):
        b = back[c]
        arrive(0, c, piece(h, 3, c))
        if c < half:
            go(3, c, piece(h, 3, c), right)
        arrive(1, b, piece(h, 1, b))
        if b >= half:
            go(3, b, piece(h, 1, b), left)
        arrive(2, c, piece(1 - h, 0, c))
        go(4, c, piece(1 - h, 0, c), right)
        go(5, c, piece(1 - h, 0, c), left)
    for c in range(CHUNKS):
        arrive(4, c, piece(1 - h, 3, c))
        if c < half:
            go(6, c, piece(1 - h, 3, c), right)
        arrive(5, c, piece(1 - h, 1, c))
        if c >= half:
            go(6, c, piece(1 - h, 1, c), left)
    for c in range(CHUNKS):
        arrive(3, c, piece(h, 2, c))
    for c in range(CHUNKS):
        arrive(6, c, piece(1 - h, 2, c))
    for op in sent:
        op.wait_send()


def tiles_kernel(rows, cols, counts, tiles, part, own, sib, acc, narrow, sems):
    step = pl.program_id(0)
    core = lax.rem(lax.axis_index("dom"), 2)
    blocks = acc.shape[0] - 1
    half = blocks // 2

    @pl.when(step == 0)
    def _():
        def clear(i, _):
            acc[i] = jnp.zeros((TILE, F), F32)
            return 0

        lax.fori_loop(0, blocks, clear, 0)

    count = counts[0]

    def one(t):
        at = step * GROUP + t
        col = cols[at]
        pair = col // BLOCKS
        away = lax.rem(lax.rem(pair, 2) + core, 2)
        slot = away * half + pair // 2 * BLOCKS + lax.rem(col, BLOCKS)
        slot = jnp.where(at < count, slot, blocks)
        acc[slot] += lax.dot_general(
            tiles[t], part[rows[at]], (((0,), (0,)), ((), ())), preferred_element_type=F32
        )

    unroll = 8

    def body(i, _):
        for u in range(unroll):
            one(i * unroll + u)
        return 0

    lax.fori_loop(0, GROUP // unroll, body, 0)

    @pl.when(step == pl.num_programs(0) - 1)
    def _():
        mine = pltpu.make_async_copy(acc.at[pl.ds(0, half)], own, sems.at[0])
        mine.start()

        def shorten(i, _):
            narrow[i] = acc[half + i].astype(BF16)
            return 0

        lax.fori_loop(0, half, shorten, 0)
        other = pltpu.make_async_copy(narrow, sib, sems.at[1])
        other.start()
        mine.wait()
        other.wait()


def scatter_kernel(
    own_hbm, sib_hbm, wpart, node, wgrad,
    own, got, relay_in, final_in, outbox, ybox, yin, w_loop, w_z, w_pair, w_zall,
    load, sib_send, sib_recv, z_send, z_recv, y_send, y_recv, w_send, w_recv,
):
    dom, loop = lax.axis_index("dom"), lax.axis_index("loop")
    z, y, core = dom // 4, lax.rem(dom // 2, 2), lax.rem(dom, 2)

    def at(zz, yy, cc):
        return {"dom": zz * 4 + yy * 2 + cc}

    def zed(k):
        return lax.rem(z + k, Z)

    sibling = at(z, y, 1 - core)
    up, far, down = at(zed(1), y, core), at(zed(2), y, core), at(zed(3), y, core)
    over = at(z, 1 - y, core)
    diagonal = at(z, 1 - y, 1 - core)
    ring = [{"loop": lax.rem(loop + k, LOOP)} for k in range(1, LOOP)]
    barrier, arrivals = greet([sibling, up, far, down, over, diagonal] + ring)

    ys = (1 - y, y)
    order = [(2, 0), (1, 0), (3, 0), (2, 1), (1, 1), (3, 1), (0, 0), (0, 1)]
    loads = {}
    for k, i in order:
        op = pltpu.make_async_copy(own_hbm.at[zed(k), ys[i]], own.at[k, i], load.at[k, i])
        op.start()
        loads[k, i] = op
    pl.semaphore_wait(barrier, arrivals)
    sent = []

    def go(op):
        op.start()
        sent.append(op)

    def sib_copy(k, i):
        return remote(sib_hbm.at[zed(k), ys[i]], got.at[k, i], sib_send.at[k, i], sib_recv.at[k, i], sibling)

    for k, i in order:
        go(sib_copy(k, i))

    thin = F // LOOP // Z

    def w_copy(src, dst, s, r, where):
        return remote(src, dst, w_send.at[s], w_recv.at[r], where)

    def w_first():
        for k in range(1, LOOP):
            peer = lax.rem(loop + k, LOOP)
            go(w_copy(wpart.at[pl.ds(peer * 32, 32)], w_loop.at[k], k, k, ring[k - 1]))

    def w_second():
        for k in range(1, LOOP):
            w_copy(w_loop.at[k], w_loop.at[k], k, k, ring[0]).wait_recv()
        total = wpart[pl.ds(pl.multiple_of(loop * 32, 32), 32)]
        for k in range(1, LOOP):
            total += w_loop[k]
        w_loop[0] = total
        for k, where in ((1, up), (2, far), (3, down)):
            go(w_copy(w_loop.at[0, pl.ds(zed(k) * thin, thin)], w_z.at[k], 7 + k, 7 + k, where))

    def w_third():
        for k in range(1, Z):
            w_copy(w_z.at[k], w_z.at[k], 7 + k, 7 + k, up).wait_recv()
        total = w_loop[0, pl.ds(pl.multiple_of(z * thin, thin), thin)]
        for k in range(1, Z):
            total += w_z[k]
        w_pair[y * 2 + core] = total
        mine = w_pair.at[y * 2 + core]
        for k, where in ((0, sibling), (1, over), (2, diagonal)):
            go(w_copy(mine, mine, 11 + k, 11 + k, where))

    def w_fourth():
        spots = ((0, y * 2 + 1 - core), (1, (1 - y) * 2 + core), (2, (1 - y) * 2 + 1 - core))
        for k, spot in spots:
            w_copy(w_pair.at[spot], w_pair.at[spot], 11 + k, 11 + k, up).wait_recv()
        total = ((w_pair[0] + w_pair[1]) + (w_pair[2] + w_pair[3])) * (1.0 / math.sqrt(ROWS * 128))
        rows = pl.ds(pl.multiple_of(z * thin, thin), thin)
        w_zall[rows] = total
        for k, where in ((1, up), (2, far), (3, down)):
            go(w_copy(w_zall.at[rows], w_zall.at[rows], 13 + k, 13 + k, where))

    def w_fifth():
        for k in range(1, Z):
            rows = pl.ds(zed(Z - k) * thin, thin)
            w_copy(w_zall.at[rows], w_zall.at[rows], 13 + k, 13 + k, up).wait_recv()
        rows = pl.ds(pl.multiple_of(loop * 32, 32), 32)
        wgrad[rows] = w_zall[...]
        for k in range(1, LOOP):
            go(w_copy(w_zall, wgrad.at[rows], 16 + k, 16 + k, ring[k - 1]))

    def w_last():
        for k in range(1, LOOP):
            rows = pl.ds(lax.rem(loop + LOOP - k, LOOP) * 32, 32)
            w_copy(w_zall, wgrad.at[rows], 16 + k, 16 + k, ring[0]).wait_recv()

    w_first()

    size = ROWS // 2
    rows = [pl.ds(0, size), pl.ds(size, size)]
    ready = set()

    def chip(k, i, p):
        if (k, i) not in ready:
            ready.add((k, i))
            loads[k, i].wait()
            sib_copy(k, i).wait_recv()
        return own[k, i, rows[p]] + got[k, i, rows[p]].astype(F32)

    def z_copy(kind, i, p, src, dst, where):
        return remote(src, dst, z_send.at[kind, i, p], z_recv.at[kind, i, p], where)

    ways = (up, down)
    near = (1, 3)

    def start_far(i):
        for p in (0, 1):
            box = outbox.at[0, i, p]
            box[...] = chip(2, i, p).astype(BF16)
            go(z_copy(0, i, p, box, relay_in.at[i, p], ways[p]))

    def start_plain(i):
        for p in (0, 1):
            box = outbox.at[1, i, p]
            box[...] = chip(near[p], i, 1 - p).astype(BF16)
            go(z_copy(1, i, p, box, final_in.at[0, i, 1 - p], ways[p]))

    def start_relayed(i):
        for p in (0, 1):
            z_copy(0, i, p, relay_in.at[i, p], relay_in.at[i, p], up).wait_recv()
            box = outbox.at[2, i, p]
            box[...] = (chip(near[p], i, p) + relay_in[i, p].astype(F32)).astype(BF16)
            go(z_copy(2, i, p, box, final_in.at[1, i, p], ways[p]))

    def finish(i, p):
        z_copy(1, i, 1 - p, final_in.at[0, i, p], final_in.at[0, i, p], up).wait_recv()
        z_copy(2, i, p, final_in.at[1, i, p], final_in.at[1, i, p], up).wait_recv()
        return chip(0, i, p) + final_in[0, i, p].astype(F32) + final_in[1, i, p].astype(F32)

    start_far(0)
    start_plain(0)
    start_far(1)
    start_relayed(0)
    w_second()
    start_plain(1)
    w_third()
    for p in (0, 1):
        ybox[p] = finish(0, p).astype(BF16)
        go(remote(ybox.at[p], yin.at[p], y_send.at[p], y_recv.at[p], over))
    w_fourth()
    start_relayed(1)
    w_fifth()
    for p in (0, 1):
        total = finish(1, p)
        remote(ybox.at[p], yin.at[p], y_send.at[p], y_recv.at[p], over).wait_recv()
        node[rows[p]] = total + yin[p].astype(F32)
    w_last()
    for op in sent:
        op.wait_send()


def shards(cotangent, preact, aggregated, weight, tile_values, tile_rows, tile_cols, tile_counts):
    params = functools.partial(pltpu.CompilerParams, vmem_limit_bytes=56 * 1024 * 1024)
    dma = pltpu.SemaphoreType.DMA
    gathered, wpart = pl.pallas_call(
        gather_kernel,
        out_shape=(
            jax.ShapeDtypeStruct((LOOP, ROWS, F), BF16),
            jax.ShapeDtypeStruct((F, F), F32),
        ),
        in_specs=[VMEM] * 4,
        out_specs=(VMEM, VMEM),
        scratch_shapes=[pltpu.VMEM((ROWS, F), BF16), dma((7, CHUNKS)), dma((7, CHUNKS))],
        compiler_params=params(collective_id=0, has_side_effects=True),
        name="gather",
    )(cotangent, preact, aggregated, weight)

    slots = tile_rows.shape[1]
    blocks = LOOP * 2 * BLOCKS
    half = blocks // 2
    own, sib = pl.pallas_call(
        tiles_kernel,
        out_shape=(
            jax.ShapeDtypeStruct((half, TILE, F), F32),
            jax.ShapeDtypeStruct((half, TILE, F), BF16),
        ),
        grid_spec=pltpu.PrefetchScalarGridSpec(
            num_scalar_prefetch=3,
            grid=(slots // GROUP,),
            in_specs=[
                pl.BlockSpec((GROUP, TILE, TILE), lambda g, *_: (g, 0, 0)),
                pl.BlockSpec((LOOP * BLOCKS, TILE, F), lambda g, *_: (0, 0, 0)),
            ],
            out_specs=(ANY, ANY),
            scratch_shapes=[
                pltpu.VMEM((blocks + 1, TILE, F), F32),
                pltpu.VMEM((half, TILE, F), BF16),
                dma((2,)),
            ],
        ),
        compiler_params=params(),
        name="tiles",
    )(tile_rows[0], tile_cols[0], tile_counts, tile_values, gathered.reshape(LOOP * BLOCKS, TILE, F))

    part = (ROWS // 2, F)
    node, wgrad = pl.pallas_call(
        scatter_kernel,
        out_shape=(
            jax.ShapeDtypeStruct((ROWS, F), F32),
            jax.ShapeDtypeStruct((F, F), F32),
        ),
        in_specs=[ANY, ANY, VMEM],
        out_specs=(VMEM, VMEM),
        scratch_shapes=[
            pltpu.VMEM((Z, 2, ROWS, F), F32),
            pltpu.VMEM((Z, 2, ROWS, F), BF16),
            pltpu.VMEM((2, 2) + part, BF16),
            pltpu.VMEM((2, 2, 2) + part, BF16),
            pltpu.VMEM((3, 2, 2) + part, BF16),
            pltpu.VMEM((2,) + part, BF16),
            pltpu.VMEM((2,) + part, BF16),
            pltpu.VMEM((LOOP, F // LOOP, F), F32),
            pltpu.VMEM((Z, F // LOOP // Z, F), F32),
            pltpu.VMEM((4, F // LOOP // Z, F), F32),
            pltpu.VMEM((F // LOOP, F), F32),
            dma((Z, 2)), dma((Z, 2)), dma((Z, 2)),
            dma((3, 2, 2)), dma((3, 2, 2)),
            dma((2,)), dma((2,)),
            dma((24,)), dma((24,)),
        ],
        compiler_params=params(collective_id=1, has_side_effects=True),
        name="scatter",
    )(own.reshape(Z, 2, ROWS, F), sib.reshape(Z, 2, ROWS, F), wpart)
    return node, wgrad


def solution(mesh):
    split = P(("dom", "loop"))
    return jax.shard_map(
        shards,
        mesh=mesh,
        in_specs=(split, split, split, P(), split, split, split, split),
        out_specs=(split, P()),
        check_vma=False,
    )
```

```python
import functools
import math

import jax
import jax.numpy as jnp
from jax import lax
from jax.experimental import pallas as pl
from jax.experimental.pallas import tpu as pltpu
from jax.sharding import PartitionSpec as P

MESH = pl.DeviceIdType.MESH
VMEM = pl.BlockSpec(memory_space=pltpu.VMEM)
ANY = pl.BlockSpec(memory_space=pl.ANY)
F32 = jnp.float32
BF16 = jnp.bfloat16

ROWS = 1024
F = 256
TILE = 128
BLOCKS = 8
X = 4
LOOP = 8
Z = 4
HALF = F // 2
CHUNKS = 4
SLOTS = 640
STEPS = (SLOTS + 64) // 2
WIDE = 768
UNROLL = 32


def remote(src, dst, send, recv, where):
    return pltpu.make_async_remote_copy(
        src_ref=src, dst_ref=dst, send_sem=send, recv_sem=recv, device_id=where, device_id_type=MESH
    )


def greet(peers):
    barrier = pltpu.get_barrier_semaphore()
    for peer in peers:
        pl.semaphore_signal(barrier, inc=1, device_id=peer, device_id_type=MESH)
    return barrier, len(peers)


def plan_kernel(rows, cols, count, out):
    blocks = 128

    def iota(shape, axis):
        return lax.broadcasted_iota(jnp.int32, shape, axis)

    def pick(mask, value, axis):
        return jnp.sum(jnp.where(mask, value, 0.0), axis=axis, keepdims=True)

    live = iota((1, SLOTS), 1) < count[0]
    hit = (iota((blocks, SLOTS), 0) == cols[...]) & live
    hits = jnp.where(hit, 1.0, 0.0)
    number = jnp.sum(hits, axis=1, keepdims=True)
    steps = jnp.floor((number + 1.0) * 0.5)
    down, along = iota((blocks, blocks), 0), iota((blocks, blocks), 1)
    steps_row = pick(down == along, steps, 0)
    first = pick(along < down, steps_row, 1)
    first_row = pick(down < along, steps, 0)
    out[3:4, 0:blocks] = jnp.where(steps_row > 0, first_row + steps_row - 1.0, float(STEPS)).astype(jnp.int32)
    out[3:4, blocks:] = jnp.zeros((1, WIDE - blocks), jnp.int32)

    big = (SLOTS, SLOTS)
    earlier = jnp.where(iota(big, 0) < iota(big, 1), 1.0, 0.0).astype(BF16)
    rank = jnp.dot(hits.astype(BF16), earlier, preferred_element_type=F32)
    place = jnp.where(live, pick(hit, 2.0 * first + rank, 0), 1000.0)
    both = place * 64.0 + rows[...].astype(F32)
    both = pick(iota(big, 0) == iota(big, 1), both, 1)
    place = jnp.floor(both * (1.0 / 64.0))
    row = both - place * 64.0
    found = place.astype(jnp.int32) == iota((SLOTS, WIDE), 1)
    tile = pick(found, iota((SLOTS, WIDE), 0).astype(F32) - float(SLOTS), 0) + float(SLOTS)
    out[0:1] = tile.astype(jnp.int32)
    out[1:2] = pick(found, row, 0).astype(jnp.int32)
    opens = (first.astype(jnp.int32) == iota((blocks, WIDE), 1)) & (steps > 0)
    out[2:3] = (1.0 - jnp.max(jnp.where(opens, 1.0, 0.0), axis=0, keepdims=True)).astype(jnp.int32)


def layer_kernel(
    plan, cot, pre, agg, w, tiles_hbm, node, wgrad,
    tiles, part_a, part_b, masked, prefix, acc, own, sibbox, got, relay_in, final_in, outbox, ybox, yin,
    wpart, w_z, w_loop, w_pair, w_all,
    tile_sem, g_send, g_recv, s_send, s_recv, z_send, z_recv, y_send, y_recv, w_send, w_recv,
):
    dom, loop = lax.axis_index("dom"), lax.axis_index("loop")
    z, y, core = dom // 4, lax.rem(dom // 2, 2), lax.rem(dom, 2)
    x, high = lax.rem(loop, X), loop // X

    def at(zz, yy, cc):
        return {"dom": zz * 4 + yy * 2 + cc}

    def zed(k):
        return lax.rem(z + k, Z)

    sibling = at(z, y, 1 - core)
    up, far, down = at(zed(1), y, core), at(zed(2), y, core), at(zed(3), y, core)
    over = at(z, 1 - y, core)
    diagonal = at(z, 1 - y, 1 - core)
    right = {"loop": high * X + lax.rem(x + 1, X)}
    left = {"loop": high * X + lax.rem(x + X - 1, X)}
    across = {"loop": (1 - high) * X + x}
    ring = [{"loop": lax.rem(loop + k, LOOP)} for k in range(1, LOOP)]
    barrier, arrivals = greet([sibling, up, far, down, over, diagonal] + ring)

    load = pltpu.make_async_copy(tiles_hbm, tiles.at[pl.ds(0, SLOTS)], tile_sem)
    load.start()
    tiles[SLOTS] = jnp.zeros((TILE, TILE), BF16)
    prefix[STEPS] = jnp.zeros((TILE, HALF), BF16)
    sent = []

    def go(op):
        op.start()
        sent.append(op)

    part = (part_a, part_b)

    count = BLOCKS // CHUNKS

    def piece(f, hh, step, c):
        return part[f].at[pl.ds((hh * X + lax.rem(x + step, X)) * BLOCKS + c * count, count)]

    def g_copy(f, kind, c, ref, where):
        return remote(ref, ref, g_send.at[f, kind, c], g_recv.at[f, kind, c], where)

    def arrive(f, kind, c, ref):
        g_copy(f, kind, c, ref, right).wait_recv()

    back = [CHUNKS - 1 - c for c in range(CHUNKS)]

    def project(f):
        for c in range(2):
            rows = pl.ds(c * (ROWS // 2), ROWS // 2)
            if f == 0:
                masked[rows] = jnp.where(pre[rows].astype(F32) > 0, cot[rows].astype(F32), 0.0).astype(BF16)
            out = lax.dot_general(
                masked[rows], w[f * HALF:(f + 1) * HALF], (((1,), (1,)), ((), ())), preferred_element_type=F32
            )
            part[f][pl.ds(loop * BLOCKS + c * (BLOCKS // 2), BLOCKS // 2)] = out.astype(BF16).reshape(
                BLOCKS // 2, TILE, HALF
            )

    def gather_own(f):
        for c in range(CHUNKS):
            go(g_copy(f, 0, c, piece(f, high, 0, c), right))
            go(g_copy(f, 1, back[c], piece(f, high, 0, back[c]), left))
            go(g_copy(f, 2, c, piece(f, high, 0, c), across))

    def gather_on(f, chunks):
        for c in chunks:
            b = back[c]
            arrive(f, 0, c, piece(f, high, 3, c))
            if c < CHUNKS // 2:
                go(g_copy(f, 3, c, piece(f, high, 3, c), right))
            arrive(f, 1, b, piece(f, high, 1, b))
            if b >= CHUNKS // 2:
                go(g_copy(f, 3, b, piece(f, high, 1, b), left))
            arrive(f, 2, c, piece(f, 1 - high, 0, c))
            go(g_copy(f, 4, c, piece(f, 1 - high, 0, c), right))
            go(g_copy(f, 5, c, piece(f, 1 - high, 0, c), left))

    def gather_last(f):
        for c in range(CHUNKS):
            arrive(f, 4, c, piece(f, 1 - high, 3, c))
            if c < CHUNKS // 2:
                go(g_copy(f, 6, c, piece(f, 1 - high, 3, c), right))
            arrive(f, 5, c, piece(f, 1 - high, 1, c))
            if c >= CHUNKS // 2:
                go(g_copy(f, 6, c, piece(f, 1 - high, 1, c), left))

    def gather_end(f):
        for c in range(CHUNKS):
            arrive(f, 3, c, piece(f, high, 2, c))
        for c in range(CHUNKS):
            arrive(f, 6, c, piece(f, 1 - high, 2, c))

    thick, thin = F // Z, F // Z // LOOP

    def w_copy(src, dst, s, where):
        return remote(src, dst, w_send.at[s], w_recv.at[s], where)

    def own_rows(ref, index, size):
        return ref.at[pl.ds(pl.multiple_of(index * size, size), size)]

    def w_first():
        total = jnp.zeros((F, F), F32)
        for c in range(4):
            rows = pl.ds(c * (ROWS // 4), ROWS // 4)
            total += lax.dot_general(
                agg[rows], masked[rows], (((0,), (0,)), ((), ())), preferred_element_type=F32
            )
        wpart[...] = total
        for k, where in ((1, up), (2, far), (3, down)):
            go(w_copy(own_rows(wpart, zed(k), thick), w_z.at[k], k, where))

    def w_second():
        for k in range(1, Z):
            w_copy(w_z.at[k], w_z.at[k], k, up).wait_recv()
        total = own_rows(wpart, z, thick)[...]
        for k in range(1, Z):
            total += w_z[k]
        w_z[0] = total
        for k in range(1, LOOP):
            go(w_copy(own_rows(w_z.at[0], lax.rem(loop + k, LOOP), thin), w_loop.at[k], 3 + k, ring[k - 1]))

    def w_third():
        for k in range(1, LOOP):
            w_copy(w_loop.at[k], w_loop.at[k], 3 + k, up).wait_recv()
        total = own_rows(w_z.at[0], loop, thin)[...]
        for k in range(1, LOOP):
            total += w_loop[k]
        w_pair[y * 2 + core] = total
        mine = w_pair.at[y * 2 + core]
        for k, where in ((0, sibling), (1, over), (2, diagonal)):
            go(w_copy(mine, mine, 11 + k, where))

    def w_fourth():
        for k, spot in ((0, y * 2 + 1 - core), (1, (1 - y) * 2 + core), (2, (1 - y) * 2 + 1 - core)):
            w_copy(w_pair.at[spot], w_pair.at[spot], 11 + k, up).wait_recv()
        total = ((w_pair[0] + w_pair[1]) + (w_pair[2] + w_pair[3])) * (1.0 / math.sqrt(ROWS * 128))
        mine = own_rows(w_all, loop, thin)
        mine[...] = total
        for k in range(1, LOOP):
            go(w_copy(mine, mine, 13 + k, ring[k - 1]))

    def w_fifth():
        for k in range(1, LOOP):
            theirs = own_rows(w_all, lax.rem(loop + LOOP - k, LOOP), thin)
            w_copy(theirs, theirs, 13 + k, up).wait_recv()
        mine = own_rows(wgrad, z, thick)
        mine[...] = w_all[...]
        for k, where in ((1, up), (2, far), (3, down)):
            go(w_copy(w_all, mine, 20 + k, where))

    def w_last():
        for k in range(1, Z):
            w_copy(w_all, own_rows(wgrad, zed(Z - k), thick), 20 + k, up).wait_recv()

    def multiply(f, start, end):
        def one(s, total):
            pair = jnp.concatenate([tiles[plan[0, 2 * s]], tiles[plan[0, 2 * s + 1]]], axis=0)
            source = jnp.concatenate([part[f][plan[1, 2 * s]], part[f][plan[1, 2 * s + 1]]], axis=0)
            term = lax.dot_general(pair, source, (((0,), (0,)), ((), ())), preferred_element_type=F32)
            total = jnp.where(plan[2, s] != 0, total, 0.0) + term
            prefix[s] = total.astype(BF16)
            return total

        begin = jnp.zeros((TILE, HALF), F32) if start == 0 else acc[...]
        acc[...] = lax.fori_loop(start, end, one, begin, unroll=UNROLL)

    ys = (1 - y, y)
    order = [(2, 0), (1, 0), (3, 0), (2, 1), (1, 1), (3, 1), (0, 0), (0, 1)]

    def s_copy(f, k, i):
        return remote(sibbox.at[f, k, i], got.at[f, k, i], s_send.at[f, k, i], s_recv.at[f, k, i], sibling)

    def extract(f, box, k, i, cc):
        base = ((zed(k) * 2 + ys[i]) * 2 + cc) * BLOCKS

        def one(b, _):
            box[f, k, i, pl.ds(pl.multiple_of(b * TILE, TILE), TILE)] = prefix[plan[3, base + b]]
            return 0

        lax.fori_loop(0, BLOCKS, one, 0, unroll=BLOCKS)

    def split(f):
        for k, i in order:
            extract(f, sibbox, k, i, 1 - core)
            go(s_copy(f, k, i))
        for k, i in order:
            extract(f, own, k, i, core)

    size = ROWS // 2
    rows = [pl.ds(0, size), pl.ds(size, size)]
    ready = set()

    def chip(f, k, i, p):
        if (f, k, i) not in ready:
            ready.add((f, k, i))
            s_copy(f, k, i).wait_recv()
        return own[f, k, i, rows[p]].astype(F32) + got[f, k, i, rows[p]].astype(F32)

    def z_copy(f, kind, i, p, src, dst, where):
        return remote(src, dst, z_send.at[f, kind, i, p], z_recv.at[f, kind, i, p], where)

    ways = (up, down)
    near = (1, 3)

    def start_far(f, i):
        for p in (0, 1):
            box = outbox.at[f, 0, i, p]
            box[...] = chip(f, 2, i, p).astype(BF16)
            go(z_copy(f, 0, i, p, box, relay_in.at[f, i, p], ways[p]))

    def start_plain(f, i):
        for p in (0, 1):
            box = outbox.at[f, 1, i, p]
            box[...] = chip(f, near[p], i, 1 - p).astype(BF16)
            go(z_copy(f, 1, i, p, box, final_in.at[f, 0, i, 1 - p], ways[p]))

    def start_relayed(f, i):
        for p in (0, 1):
            z_copy(f, 0, i, p, relay_in.at[f, i, p], relay_in.at[f, i, p], up).wait_recv()
            box = outbox.at[f, 2, i, p]
            box[...] = (chip(f, near[p], i, p) + relay_in[f, i, p].astype(F32)).astype(BF16)
            go(z_copy(f, 2, i, p, box, final_in.at[f, 1, i, p], ways[p]))

    def finish(f, i, p):
        z_copy(f, 1, i, 1 - p, final_in.at[f, 0, i, p], final_in.at[f, 0, i, p], up).wait_recv()
        z_copy(f, 2, i, p, final_in.at[f, 1, i, p], final_in.at[f, 1, i, p], up).wait_recv()
        return chip(f, 0, i, p) + final_in[f, 0, i, p].astype(F32) + final_in[f, 1, i, p].astype(F32)

    def y_copy(f, p):
        return remote(ybox.at[f, p], yin.at[f, p], y_send.at[f, p], y_recv.at[f, p], over)

    def start_y(f):
        for p in (0, 1):
            ybox[f, p] = finish(f, 0, p).astype(BF16)
            go(y_copy(f, p))

    def end(f):
        for p in (0, 1):
            total = finish(f, 1, p)
            y_copy(f, p).wait_recv()
            node[rows[p], f * HALF:(f + 1) * HALF] = total + yin[f, p].astype(F32)

    cut = [0, 128, 256, STEPS]
    project(0)
    pl.semaphore_wait(barrier, arrivals)
    gather_own(0)
    project(1)
    w_first()
    gather_on(0, range(CHUNKS))
    w_second()
    gather_last(0)
    gather_own(1)
    w_third()
    gather_end(0)
    w_fourth()
    load.wait()
    multiply(0, cut[0], cut[1])
    w_fifth()
    multiply(0, cut[1], cut[2])
    gather_on(1, range(CHUNKS))
    multiply(0, cut[2], cut[3])
    split(0)
    gather_last(1)
    start_far(0, 0)
    start_plain(0, 0)
    start_far(0, 1)
    start_relayed(0, 0)
    start_plain(0, 1)
    gather_end(1)
    multiply(1, cut[0], cut[1])
    start_relayed(0, 1)
    multiply(1, cut[1], cut[2])
    start_y(0)
    multiply(1, cut[2], cut[3])
    split(1)
    start_far(1, 0)
    start_plain(1, 0)
    start_far(1, 1)
    end(0)
    start_relayed(1, 0)
    start_plain(1, 1)
    start_y(1)
    start_relayed(1, 1)
    end(1)
    w_last()
    for op in sent:
        op.wait_send()


def shards(cotangent, preact, aggregated, weight, tile_values, tile_rows, tile_cols, tile_counts):
    dma = pltpu.SemaphoreType.DMA
    SMEM = pl.BlockSpec(memory_space=pltpu.SMEM)
    plan = pl.pallas_call(
        plan_kernel,
        out_shape=jax.ShapeDtypeStruct((4, WIDE), jnp.int32),
        in_specs=[VMEM, VMEM, SMEM],
        out_specs=VMEM,
        name="plan",
    )(tile_rows, tile_cols, tile_counts)

    size = (ROWS // 2, HALF)
    thick, thin = F // Z, F // Z // LOOP
    node, wgrad = pl.pallas_call(
        layer_kernel,
        out_shape=(
            jax.ShapeDtypeStruct((ROWS, F), F32),
            jax.ShapeDtypeStruct((F, F), F32),
        ),
        in_specs=[SMEM] + [VMEM] * 4 + [ANY],
        out_specs=(VMEM, VMEM),
        scratch_shapes=[
            pltpu.VMEM((SLOTS + 1, TILE, TILE), BF16),
            pltpu.VMEM((LOOP * BLOCKS, TILE, HALF), BF16),
            pltpu.VMEM((LOOP * BLOCKS, TILE, HALF), BF16),
            pltpu.VMEM((ROWS, F), BF16),
            pltpu.VMEM((STEPS + 1, TILE, HALF), BF16),
            pltpu.VMEM((TILE, HALF), F32),
            pltpu.VMEM((2, Z, 2, ROWS, HALF), BF16),
            pltpu.VMEM((2, Z, 2, ROWS, HALF), BF16),
            pltpu.VMEM((2, Z, 2, ROWS, HALF), BF16),
            pltpu.VMEM((2, 2, 2) + size, BF16),
            pltpu.VMEM((2, 2, 2, 2) + size, BF16),
            pltpu.VMEM((2, 3, 2, 2) + size, BF16),
            pltpu.VMEM((2, 2) + size, BF16),
            pltpu.VMEM((2, 2) + size, BF16),
            pltpu.VMEM((F, F), F32),
            pltpu.VMEM((Z, thick, F), F32),
            pltpu.VMEM((LOOP, thin, F), F32),
            pltpu.VMEM((4, thin, F), F32),
            pltpu.VMEM((thick, F), F32),
            dma,
            dma((2, 7, CHUNKS)), dma((2, 7, CHUNKS)),
            dma((2, Z, 2)), dma((2, Z, 2)),
            dma((2, 3, 2, 2)), dma((2, 3, 2, 2)),
            dma((2, 2)), dma((2, 2)),
            dma((24,)), dma((24,)),
        ],
        compiler_params=pltpu.CompilerParams(
            vmem_limit_bytes=60 * 1024 * 1024, collective_id=0, has_side_effects=True
        ),
        name="layer",
    )(plan, cotangent, preact, aggregated, weight, tile_values)
    return node, wgrad


def solution(mesh):
    split = P(("dom", "loop"))
    return jax.shard_map(
        shards,
        mesh=mesh,
        in_specs=(split, split, split, P(), split, split, split, split),
        out_specs=(split, P()),
        check_vma=False,
    )
```

```python
import functools
import math

import jax
import jax.numpy as jnp
from jax import lax
from jax.experimental import pallas as pl
from jax.experimental.pallas import tpu as pltpu
from jax.sharding import PartitionSpec as P

MESH = pl.DeviceIdType.MESH
VMEM = pl.BlockSpec(memory_space=pltpu.VMEM)
ANY = pl.BlockSpec(memory_space=pl.ANY)
F32 = jnp.float32
BF16 = jnp.bfloat16

ROWS = 1024
F = 256
TILE = 128
BLOCKS = 8
X = 4
LOOP = 8
Z = 4
HALF = F // 2
CHUNKS = 4
SLOTS = 640
STEPS = (SLOTS + 64) // 2
WIDE = 768
UNROLL = 88
CROSS = ((1, 2), (1,))


def remote(src, dst, send, recv, where):
    return pltpu.make_async_remote_copy(
        src_ref=src, dst_ref=dst, send_sem=send, recv_sem=recv, device_id=where, device_id_type=MESH
    )


def greet(peers):
    barrier = pltpu.get_barrier_semaphore()
    for peer in peers:
        pl.semaphore_signal(barrier, inc=1, device_id=peer, device_id_type=MESH)
    return barrier, len(peers)


def plan_kernel(rows, cols, count, out):
    blocks = 128

    def iota(shape, axis):
        return lax.broadcasted_iota(jnp.int32, shape, axis)

    def pick(mask, value, axis):
        return jnp.sum(jnp.where(mask, value, 0.0), axis=axis, keepdims=True)

    live = iota((1, SLOTS), 1) < count[0]
    hit = (iota((blocks, SLOTS), 0) == cols[...]) & live
    hits = jnp.where(hit, 1.0, 0.0)
    number = jnp.sum(hits, axis=1, keepdims=True)
    steps = jnp.floor((number + 1.0) * 0.5)
    down, along = iota((blocks, blocks), 0), iota((blocks, blocks), 1)
    steps_row = pick(down == along, steps, 0)
    first = pick(along < down, steps_row, 1)
    first_row = pick(down < along, steps, 0)
    out[3:4, 0:blocks] = jnp.where(steps_row > 0, first_row + steps_row - 1.0, float(STEPS)).astype(jnp.int32)
    out[3:4, blocks:] = jnp.zeros((1, WIDE - blocks), jnp.int32)

    big = (SLOTS, SLOTS)
    earlier = jnp.where(iota(big, 0) < iota(big, 1), 1.0, 0.0).astype(BF16)
    rank = jnp.dot(hits.astype(BF16), earlier, preferred_element_type=F32)
    place = jnp.where(live, pick(hit, 2.0 * first + rank, 0), 1000.0)
    both = place * 64.0 + rows[...].astype(F32)
    both = pick(iota(big, 0) == iota(big, 1), both, 1)
    place = jnp.floor(both * (1.0 / 64.0))
    row = both - place * 64.0
    found = place.astype(jnp.int32) == iota((SLOTS, WIDE), 1)
    tile = pick(found, iota((SLOTS, WIDE), 0).astype(F32) - float(SLOTS), 0) + float(SLOTS)
    out[0:1] = tile.astype(jnp.int32)
    out[1:2] = pick(found, row, 0).astype(jnp.int32)
    opens = (first.astype(jnp.int32) == iota((blocks, WIDE), 1)) & (steps > 0)
    out[2:3] = (1.0 - jnp.max(jnp.where(opens, 1.0, 0.0), axis=0, keepdims=True)).astype(jnp.int32)


def layer_kernel(
    plan, cot, pre, agg, w, tiles_hbm, node, wgrad,
    tiles, part_a, part_b, masked, prefix, acc, own, sibbox, got, relay_in, final_in, outbox, ybox, yin,
    wpart, w_z, w_loop, w_pair, w_all,
    tile_sem, g_send, g_recv, s_send, s_recv, z_send, z_recv, y_send, y_recv, w_send, w_recv,
):
    dom, loop = lax.axis_index("dom"), lax.axis_index("loop")
    z, y, core = dom // 4, lax.rem(dom // 2, 2), lax.rem(dom, 2)
    x, high = lax.rem(loop, X), loop // X

    def at(zz, yy, cc):
        return {"dom": zz * 4 + yy * 2 + cc}

    def zed(k):
        return lax.rem(z + k, Z)

    sibling = at(z, y, 1 - core)
    up, far, down = at(zed(1), y, core), at(zed(2), y, core), at(zed(3), y, core)
    over = at(z, 1 - y, core)
    diagonal = at(z, 1 - y, 1 - core)
    right = {"loop": high * X + lax.rem(x + 1, X)}
    left = {"loop": high * X + lax.rem(x + X - 1, X)}
    across = {"loop": (1 - high) * X + x}
    ring = [{"loop": lax.rem(loop + k, LOOP)} for k in range(1, LOOP)]
    barrier, arrivals = greet([sibling, up, far, down, over, diagonal] + ring)

    load = pltpu.make_async_copy(tiles_hbm, tiles.at[pl.ds(0, SLOTS)], tile_sem)
    load.start()
    tiles[SLOTS] = jnp.zeros((TILE, TILE), BF16)
    prefix[STEPS] = jnp.zeros((TILE, HALF), BF16)
    sent = []

    def go(op):
        op.start()
        sent.append(op)

    part = (part_a, part_b)

    count = BLOCKS // CHUNKS

    def piece(f, hh, step, c):
        return part[f].at[pl.ds((hh * X + lax.rem(x + step, X)) * BLOCKS + c * count, count)]

    def g_copy(f, kind, c, ref, where):
        return remote(ref, ref, g_send.at[f, kind, c], g_recv.at[f, kind, c], where)

    def arrive(f, kind, c, ref):
        g_copy(f, kind, c, ref, right).wait_recv()

    back = [CHUNKS - 1 - c for c in range(CHUNKS)]

    def project(f):
        for c in range(2):
            rows = pl.ds(c * (ROWS // 2), ROWS // 2)
            if f == 0:
                masked[rows] = jnp.where(pre[rows].astype(F32) > 0, cot[rows].astype(F32), 0.0).astype(BF16)
            out = lax.dot_general(
                w[f * HALF:(f + 1) * HALF], masked[rows], (((1,), (1,)), ((), ())), preferred_element_type=F32
            ).astype(BF16)
            for b in range(BLOCKS // 2):
                part[f][loop * BLOCKS + c * (BLOCKS // 2) + b] = out[:, b * TILE:(b + 1) * TILE]

    def gather_own(f):
        for c, b, a in zip(range(CHUNKS), back, crossing(f)):
            go(g_copy(f, 0, c, piece(f, high, 0, c), right))
            go(g_copy(f, 1, b, piece(f, high, 0, b), left))
            go(g_copy(f, 2, a, piece(f, high, 0, a), across))

    def crossing(f):
        return sorted(range(CHUNKS), key=lambda c: c in CROSS[f])

    def gather_on(f, turns):
        for n in turns:
            c, b, a = n, back[n], crossing(f)[n]
            arrive(f, 0, c, piece(f, high, 3, c))
            if c < CHUNKS // 2:
                go(g_copy(f, 3, c, piece(f, high, 3, c), right))
            if c in CROSS[f]:
                go(g_copy(f, 4, c, piece(f, high, 3, c), across))
            arrive(f, 1, b, piece(f, high, 1, b))
            if b >= CHUNKS // 2:
                go(g_copy(f, 3, b, piece(f, high, 1, b), left))
            if b in CROSS[f]:
                go(g_copy(f, 5, b, piece(f, high, 1, b), across))
            arrive(f, 2, a, piece(f, 1 - high, 0, a))
            if a not in CROSS[f]:
                go(g_copy(f, 4, a, piece(f, 1 - high, 0, a), right))
                go(g_copy(f, 5, a, piece(f, 1 - high, 0, a), left))

    def gather_last(f):
        for c in CROSS[f]:
            arrive(f, 3, c, piece(f, high, 2, c))
            go(g_copy(f, 6, c, piece(f, high, 2, c), across))
        for c in range(CHUNKS):
            if c in CROSS[f]:
                continue
            arrive(f, 4, c, piece(f, 1 - high, 3, c))
            if c < CHUNKS // 2:
                go(g_copy(f, 6, c, piece(f, 1 - high, 3, c), right))
            arrive(f, 5, c, piece(f, 1 - high, 1, c))
            if c >= CHUNKS // 2:
                go(g_copy(f, 6, c, piece(f, 1 - high, 1, c), left))

    def gather_end(f):
        for c in range(CHUNKS):
            if c in CROSS[f]:
                arrive(f, 4, c, piece(f, 1 - high, 3, c))
                arrive(f, 5, c, piece(f, 1 - high, 1, c))
            else:
                arrive(f, 3, c, piece(f, high, 2, c))
            arrive(f, 6, c, piece(f, 1 - high, 2, c))

    thick, thin = F // Z, F // Z // LOOP

    def w_copy(src, dst, s, where):
        return remote(src, dst, w_send.at[s], w_recv.at[s], where)

    def own_rows(ref, index, size):
        return ref.at[pl.ds(pl.multiple_of(index * size, size), size)]

    def w_term(c):
        rows = pl.ds(c * (ROWS // 4), ROWS // 4)
        term = lax.dot_general(
            agg[rows], masked[rows], (((0,), (0,)), ((), ())), preferred_element_type=F32
        )
        wpart[...] = term if c == 0 else wpart[...] + term

    def w_first():
        for k, where in ((1, up), (2, far), (3, down)):
            go(w_copy(own_rows(wpart, zed(k), thick), w_z.at[k], k, where))

    def w_second():
        for k in range(1, Z):
            w_copy(w_z.at[k], w_z.at[k], k, up).wait_recv()
        total = own_rows(wpart, z, thick)[...]
        for k in range(1, Z):
            total += w_z[k]
        w_z[0] = total
        for k in range(1, LOOP):
            go(w_copy(own_rows(w_z.at[0], lax.rem(loop + k, LOOP), thin), w_loop.at[k], 3 + k, ring[k - 1]))

    def w_third():
        for k in range(1, LOOP):
            w_copy(w_loop.at[k], w_loop.at[k], 3 + k, up).wait_recv()
        total = own_rows(w_z.at[0], loop, thin)[...]
        for k in range(1, LOOP):
            total += w_loop[k]
        w_pair[y * 2 + core] = total
        mine = w_pair.at[y * 2 + core]
        for k, where in ((0, sibling), (1, over), (2, diagonal)):
            go(w_copy(mine, mine, 11 + k, where))

    def w_fourth():
        for k, spot in ((0, y * 2 + 1 - core), (1, (1 - y) * 2 + core), (2, (1 - y) * 2 + 1 - core)):
            w_copy(w_pair.at[spot], w_pair.at[spot], 11 + k, up).wait_recv()
        total = ((w_pair[0] + w_pair[1]) + (w_pair[2] + w_pair[3])) * (1.0 / math.sqrt(ROWS * 128))
        mine = own_rows(w_all, loop, thin)
        mine[...] = total
        for k in range(1, LOOP):
            go(w_copy(mine, mine, 13 + k, ring[k - 1]))

    def w_fifth():
        for k in range(1, LOOP):
            theirs = own_rows(w_all, lax.rem(loop + LOOP - k, LOOP), thin)
            w_copy(theirs, theirs, 13 + k, up).wait_recv()
        mine = own_rows(wgrad, z, thick)
        mine[...] = w_all[...]
        for k, where in ((1, up), (2, far), (3, down)):
            go(w_copy(w_all, mine, 20 + k, where))

    def w_last():
        for k in range(1, Z):
            w_copy(w_all, own_rows(wgrad, zed(Z - k), thick), 20 + k, up).wait_recv()

    def multiply(f, start, end):
        def one(s, total):
            pair = jnp.concatenate([tiles[plan[0, 2 * s]], tiles[plan[0, 2 * s + 1]]], axis=0)
            source = jnp.concatenate([part[f][plan[1, 2 * s]], part[f][plan[1, 2 * s + 1]]], axis=1)
            term = jnp.dot(source, pair, preferred_element_type=F32)
            total = jnp.where(plan[2, s] != 0, total, 0.0) + term
            prefix[s] = total.astype(BF16)
            return total

        begin = jnp.zeros((HALF, TILE), F32) if start == 0 else acc[...]
        acc[...] = lax.fori_loop(start, end, one, begin, unroll=UNROLL)

    ys = (1 - y, y)
    order = [(2, 0), (1, 0), (3, 0), (2, 1), (1, 1), (3, 1), (0, 0), (0, 1)]

    def s_copy(f, k, i):
        return remote(sibbox.at[f, k, i], got.at[f, k, i], s_send.at[f, k, i], s_recv.at[f, k, i], sibling)

    def extract(f, box, k, i, cc):
        base = ((zed(k) * 2 + ys[i]) * 2 + cc) * BLOCKS

        def one(b, _):
            box[f, k, i, pl.ds(pl.multiple_of(b * TILE, TILE), TILE)] = prefix[plan[3, base + b]]
            return 0

        lax.fori_loop(0, BLOCKS, one, 0, unroll=BLOCKS)

    def split(f):
        for k, i in order:
            extract(f, sibbox, k, i, 1 - core)
            go(s_copy(f, k, i))
        for k, i in order:
            extract(f, own, k, i, core)

    size = ROWS // 2
    rows = [pl.ds(0, size), pl.ds(size, size)]
    ready = set()

    def chip(f, k, i, p):
        if (f, k, i) not in ready:
            ready.add((f, k, i))
            s_copy(f, k, i).wait_recv()
        return own[f, k, i, rows[p]].astype(F32) + got[f, k, i, rows[p]].astype(F32)

    def z_copy(f, kind, i, p, src, dst, where):
        return remote(src, dst, z_send.at[f, kind, i, p], z_recv.at[f, kind, i, p], where)

    ways = (up, down)
    near = (1, 3)

    def start_far(f, i):
        for p in (0, 1):
            box = outbox.at[f, 0, i, p]
            box[...] = chip(f, 2, i, p).astype(BF16)
            go(z_copy(f, 0, i, p, box, relay_in.at[f, i, p], ways[p]))

    def start_plain(f, i):
        for p in (0, 1):
            box = outbox.at[f, 1, i, p]
            box[...] = chip(f, near[p], i, 1 - p).astype(BF16)
            go(z_copy(f, 1, i, p, box, final_in.at[f, 0, i, 1 - p], ways[p]))

    def start_relayed(f, i):
        for p in (0, 1):
            z_copy(f, 0, i, p, relay_in.at[f, i, p], relay_in.at[f, i, p], up).wait_recv()
            box = outbox.at[f, 2, i, p]
            box[...] = (chip(f, near[p], i, p) + relay_in[f, i, p].astype(F32)).astype(BF16)
            go(z_copy(f, 2, i, p, box, final_in.at[f, 1, i, p], ways[p]))

    def finish(f, i, p):
        z_copy(f, 1, i, 1 - p, final_in.at[f, 0, i, p], final_in.at[f, 0, i, p], up).wait_recv()
        z_copy(f, 2, i, p, final_in.at[f, 1, i, p], final_in.at[f, 1, i, p], up).wait_recv()
        return chip(f, 0, i, p) + final_in[f, 0, i, p].astype(F32) + final_in[f, 1, i, p].astype(F32)

    def y_copy(f, p):
        return remote(ybox.at[f, p], yin.at[f, p], y_send.at[f, p], y_recv.at[f, p], over)

    def start_y(f):
        for p in (0, 1):
            ybox[f, p] = finish(f, 0, p).astype(BF16)
            go(y_copy(f, p))

    def end(f):
        for p in (0, 1):
            total = finish(f, 1, p)
            y_copy(f, p).wait_recv()
            total += yin[f, p].astype(F32)
            for b in range(BLOCKS // 2):
                place = pl.ds((p * (BLOCKS // 2) + b) * TILE, TILE)
                node[place, f * HALF:(f + 1) * HALF] = total[b * TILE:(b + 1) * TILE].T

    cut = [0, STEPS // 2, STEPS]
    project(0)
    pl.semaphore_wait(barrier, arrivals)
    gather_own(0)
    project(1)
    for c in range(CHUNKS):
        w_term(c)
        gather_on(0, [c])
    w_first()
    gather_last(0)
    gather_own(1)
    gather_end(0)
    load.wait()
    multiply(0, cut[0], cut[1])
    w_second()
    gather_on(1, range(CHUNKS))
    multiply(0, cut[1], cut[2])
    split(0)
    w_third()
    gather_last(1)
    start_far(0, 0)
    start_plain(0, 0)
    start_far(0, 1)
    start_relayed(0, 0)
    start_plain(0, 1)
    gather_end(1)
    w_fourth()
    multiply(1, cut[0], cut[1])
    start_relayed(0, 1)
    start_y(0)
    w_fifth()
    multiply(1, cut[1], cut[2])
    split(1)
    start_far(1, 0)
    start_plain(1, 0)
    start_far(1, 1)
    end(0)
    start_relayed(1, 0)
    start_plain(1, 1)
    start_y(1)
    start_relayed(1, 1)
    end(1)
    w_last()
    for op in sent:
        op.wait_send()


def copy_kernel(node, wgrad, node_out, wgrad_out, sem):
    rows = ROWS // 4
    ops = [pltpu.make_async_copy(wgrad, wgrad_out, sem.at[4])]
    for c in range(4):
        part = pl.ds(c * rows, rows)
        ops.append(pltpu.make_async_copy(node.at[part], node_out.at[part], sem.at[c]))
    for op in ops:
        op.start()
    for op in ops:
        op.wait()


def shards(cotangent, preact, aggregated, weight, tile_values, tile_rows, tile_cols, tile_counts):
    dma = pltpu.SemaphoreType.DMA
    SMEM = pl.BlockSpec(memory_space=pltpu.SMEM)
    plan = pl.pallas_call(
        plan_kernel,
        out_shape=jax.ShapeDtypeStruct((4, WIDE), jnp.int32),
        in_specs=[VMEM, VMEM, SMEM],
        out_specs=VMEM,
        name="plan",
    )(tile_rows, tile_cols, tile_counts)

    size = (ROWS // 2, HALF)
    thick, thin = F // Z, F // Z // LOOP
    node, wgrad = pl.pallas_call(
        layer_kernel,
        out_shape=(
            jax.ShapeDtypeStruct((ROWS, F), F32),
            jax.ShapeDtypeStruct((F, F), F32),
        ),
        in_specs=[SMEM] + [VMEM] * 4 + [ANY],
        out_specs=(VMEM, VMEM),
        scratch_shapes=[
            pltpu.VMEM((SLOTS + 1, TILE, TILE), BF16),
            pltpu.VMEM((LOOP * BLOCKS, TILE, HALF), BF16),
            pltpu.VMEM((LOOP * BLOCKS, TILE, HALF), BF16),
            pltpu.VMEM((ROWS, F), BF16),
            pltpu.VMEM((STEPS + 1, TILE, HALF), BF16),
            pltpu.VMEM((TILE, HALF), F32),
            pltpu.VMEM((2, Z, 2, ROWS, HALF), BF16),
            pltpu.VMEM((2, Z, 2, ROWS, HALF), BF16),
            pltpu.VMEM((2, Z, 2, ROWS, HALF), BF16),
            pltpu.VMEM((2, 2, 2) + size, BF16),
            pltpu.VMEM((2, 2, 2, 2) + size, BF16),
            pltpu.VMEM((2, 3, 2, 2) + size, BF16),
            pltpu.VMEM((2, 2) + size, BF16),
            pltpu.VMEM((2, 2) + size, BF16),
            pltpu.VMEM((F, F), F32),
            pltpu.VMEM((Z, thick, F), F32),
            pltpu.VMEM((LOOP, thin, F), F32),
            pltpu.VMEM((4, thin, F), F32),
            pltpu.VMEM((thick, F), F32),
            dma,
            dma((2, 7, CHUNKS)), dma((2, 7, CHUNKS)),
            dma((2, Z, 2)), dma((2, Z, 2)),
            dma((2, 3, 2, 2)), dma((2, 3, 2, 2)),
            dma((2, 2)), dma((2, 2)),
            dma((24,)), dma((24,)),
        ],
        compiler_params=pltpu.CompilerParams(
            vmem_limit_bytes=60 * 1024 * 1024, collective_id=0, has_side_effects=True
        ),
        name="layer",
    )(plan, cotangent, preact, aggregated, weight, tile_values)
    return pl.pallas_call(
        copy_kernel,
        out_shape=(
            jax.ShapeDtypeStruct((ROWS, F), F32),
            jax.ShapeDtypeStruct((F, F), F32),
        ),
        in_specs=[ANY, ANY],
        out_specs=(ANY, ANY),
        scratch_shapes=[dma((5,))],
        name="copies",
    )(node, wgrad)


def solution(mesh):
    split = P(("dom", "loop"))
    return jax.shard_map(
        shards,
        mesh=mesh,
        in_specs=(split, split, split, P(), split, split, split, split),
        out_specs=(split, P()),
        check_vma=False,
    )
```

```python
import functools
import math

import jax
import jax.numpy as jnp
from jax import lax
from jax.experimental import pallas as pl
from jax.experimental.pallas import tpu as pltpu
from jax.sharding import PartitionSpec as P

MESH = pl.DeviceIdType.MESH
VMEM = pl.BlockSpec(memory_space=pltpu.VMEM)
ANY = pl.BlockSpec(memory_space=pl.ANY)
F32 = jnp.float32
BF16 = jnp.bfloat16

ROWS = 1024
F = 256
TILE = 128
BLOCKS = 8
X = 4
LOOP = 8
Z = 4
HALF = F // 2
CHUNKS = 4
SLOTS = 640
STEPS = (SLOTS + 64) // 2
WIDE = 768
UNROLL = 88
CROSS = ((1, 2), (1,))


def remote(src, dst, send, recv, where):
    return pltpu.make_async_remote_copy(
        src_ref=src, dst_ref=dst, send_sem=send, recv_sem=recv, device_id=where, device_id_type=MESH
    )


def greet(peers):
    barrier = pltpu.get_barrier_semaphore()
    for peer in peers:
        pl.semaphore_signal(barrier, inc=1, device_id=peer, device_id_type=MESH)
    return barrier, len(peers)


def plan_kernel(rows, cols, count, out):
    blocks = 128

    def iota(shape, axis):
        return lax.broadcasted_iota(jnp.int32, shape, axis)

    def pick(mask, value, axis):
        return jnp.sum(jnp.where(mask, value, 0.0), axis=axis, keepdims=True)

    live = iota((1, SLOTS), 1) < count[0]
    hit = (iota((blocks, SLOTS), 0) == cols[...]) & live
    hits = jnp.where(hit, 1.0, 0.0)
    number = jnp.sum(hits, axis=1, keepdims=True)
    steps = jnp.floor((number + 1.0) * 0.5)
    down, along = iota((blocks, blocks), 0), iota((blocks, blocks), 1)
    steps_row = pick(down == along, steps, 0)
    first = pick(along < down, steps_row, 1)
    first_row = pick(down < along, steps, 0)
    out[3:4, 0:blocks] = jnp.where(steps_row > 0, first_row + steps_row - 1.0, float(STEPS)).astype(jnp.int32)
    out[3:4, blocks:] = jnp.zeros((1, WIDE - blocks), jnp.int32)

    big = (SLOTS, SLOTS)
    earlier = jnp.where(iota(big, 0) < iota(big, 1), 1.0, 0.0).astype(BF16)
    rank = jnp.dot(hits.astype(BF16), earlier, preferred_element_type=F32)
    place = jnp.where(live, pick(hit, 2.0 * first + rank, 0), 1000.0)
    both = place * 64.0 + rows[...].astype(F32)
    both = pick(iota(big, 0) == iota(big, 1), both, 1)
    place = jnp.floor(both * (1.0 / 64.0))
    row = both - place * 64.0
    found = place.astype(jnp.int32) == iota((SLOTS, WIDE), 1)
    tile = pick(found, iota((SLOTS, WIDE), 0).astype(F32) - float(SLOTS), 0) + float(SLOTS)
    out[0:1] = tile.astype(jnp.int32)
    out[1:2] = pick(found, row, 0).astype(jnp.int32)
    opens = (first.astype(jnp.int32) == iota((blocks, WIDE), 1)) & (steps > 0)
    out[2:3] = (1.0 - jnp.max(jnp.where(opens, 1.0, 0.0), axis=0, keepdims=True)).astype(jnp.int32)


def layer_kernel(
    plan, cot, pre, agg, w, tiles_hbm, node, wgrad,
    tiles, part_a, part_b, masked, prefix, acc, own, sibbox, got, relay_in, final_in, outbox, ybox, yin, xbox, xin,
    wpart, w_z, w_loop, w_pair, w_all,
    tile_sem, g_send, g_recv, s_send, s_recv, z_send, z_recv, y_send, y_recv, x_send, x_recv, w_send, w_recv,
):
    dom, loop = lax.axis_index("dom"), lax.axis_index("loop")
    z, y, core = dom // 4, lax.rem(dom // 2, 2), lax.rem(dom, 2)
    x, high = lax.rem(loop, X), loop // X

    def at(zz, yy, cc):
        return {"dom": zz * 4 + yy * 2 + cc}

    def zed(k):
        return lax.rem(z + k, Z)

    sibling = at(z, y, 1 - core)
    up, far, down = at(zed(1), y, core), at(zed(2), y, core), at(zed(3), y, core)
    over = at(z, 1 - y, core)
    diagonal = at(z, 1 - y, 1 - core)
    right = {"loop": high * X + lax.rem(x + 1, X)}
    left = {"loop": high * X + lax.rem(x + X - 1, X)}
    across = {"loop": (1 - high) * X + x}
    ring = [{"loop": lax.rem(loop + k, LOOP)} for k in range(1, LOOP)]
    barrier, arrivals = greet([sibling, up, far, down, over, diagonal] + ring)

    load = pltpu.make_async_copy(tiles_hbm, tiles.at[pl.ds(0, SLOTS)], tile_sem)
    load.start()
    tiles[SLOTS] = jnp.zeros((TILE, TILE), BF16)
    prefix[STEPS] = jnp.zeros((TILE, HALF), BF16)
    sent = []

    def go(op):
        op.start()
        sent.append(op)

    part = (part_a, part_b)

    count = BLOCKS // CHUNKS

    def piece(f, hh, step, c):
        return part[f].at[pl.ds((hh * X + lax.rem(x + step, X)) * BLOCKS + c * count, count)]

    def g_copy(f, kind, c, ref, where):
        return remote(ref, ref, g_send.at[f, kind, c], g_recv.at[f, kind, c], where)

    def arrive(f, kind, c, ref):
        g_copy(f, kind, c, ref, right).wait_recv()

    back = [CHUNKS - 1 - c for c in range(CHUNKS)]

    def project(f):
        for c in range(2):
            rows = pl.ds(c * (ROWS // 2), ROWS // 2)
            if f == 0:
                masked[rows] = jnp.where(pre[rows].astype(F32) > 0, cot[rows].astype(F32), 0.0).astype(BF16)
            out = lax.dot_general(
                w[f * HALF:(f + 1) * HALF], masked[rows], (((1,), (1,)), ((), ())), preferred_element_type=F32
            ).astype(BF16)
            for b in range(BLOCKS // 2):
                part[f][loop * BLOCKS + c * (BLOCKS // 2) + b] = out[:, b * TILE:(b + 1) * TILE]

    def gather_own(f):
        for c, b, a in zip(range(CHUNKS), back, crossing(f)):
            go(g_copy(f, 0, c, piece(f, high, 0, c), right))
            go(g_copy(f, 1, b, piece(f, high, 0, b), left))
            go(g_copy(f, 2, a, piece(f, high, 0, a), across))

    def crossing(f):
        return sorted(range(CHUNKS), key=lambda c: c in CROSS[f])

    def gather_on(f, turns):
        for n in turns:
            c, b, a = n, back[n], crossing(f)[n]
            arrive(f, 0, c, piece(f, high, 3, c))
            if c < CHUNKS // 2:
                go(g_copy(f, 3, c, piece(f, high, 3, c), right))
            if c in CROSS[f]:
                go(g_copy(f, 4, c, piece(f, high, 3, c), across))
            arrive(f, 1, b, piece(f, high, 1, b))
            if b >= CHUNKS // 2:
                go(g_copy(f, 3, b, piece(f, high, 1, b), left))
            if b in CROSS[f]:
                go(g_copy(f, 5, b, piece(f, high, 1, b), across))
            arrive(f, 2, a, piece(f, 1 - high, 0, a))
            if a not in CROSS[f]:
                go(g_copy(f, 4, a, piece(f, 1 - high, 0, a), right))
                go(g_copy(f, 5, a, piece(f, 1 - high, 0, a), left))

    def gather_last(f):
        for c in CROSS[f]:
            arrive(f, 3, c, piece(f, high, 2, c))
            go(g_copy(f, 6, c, piece(f, high, 2, c), across))
        for c in range(CHUNKS):
            if c in CROSS[f]:
                continue
            arrive(f, 4, c, piece(f, 1 - high, 3, c))
            if c < CHUNKS // 2:
                go(g_copy(f, 6, c, piece(f, 1 - high, 3, c), right))
            arrive(f, 5, c, piece(f, 1 - high, 1, c))
            if c >= CHUNKS // 2:
                go(g_copy(f, 6, c, piece(f, 1 - high, 1, c), left))

    def gather_end(f):
        for c in range(CHUNKS):
            if c in CROSS[f]:
                arrive(f, 4, c, piece(f, 1 - high, 3, c))
                arrive(f, 5, c, piece(f, 1 - high, 1, c))
            else:
                arrive(f, 3, c, piece(f, high, 2, c))
            arrive(f, 6, c, piece(f, 1 - high, 2, c))

    thick, thin = F // Z, F // Z // LOOP

    def w_copy(src, dst, s, where):
        return remote(src, dst, w_send.at[s], w_recv.at[s], where)

    def own_rows(ref, index, size):
        return ref.at[pl.ds(pl.multiple_of(index * size, size), size)]

    def w_term(c):
        rows = pl.ds(c * (ROWS // 4), ROWS // 4)
        term = lax.dot_general(
            agg[rows], masked[rows], (((0,), (0,)), ((), ())), preferred_element_type=F32
        )
        wpart[...] = term if c == 0 else wpart[...] + term

    def w_first():
        for k, where in ((1, up), (2, far), (3, down)):
            go(w_copy(own_rows(wpart, zed(k), thick), w_z.at[k], k, where))

    def w_second():
        for k in range(1, Z):
            w_copy(w_z.at[k], w_z.at[k], k, up).wait_recv()
        total = own_rows(wpart, z, thick)[...]
        for k in range(1, Z):
            total += w_z[k]
        w_z[0] = total
        for k in range(1, LOOP):
            go(w_copy(own_rows(w_z.at[0], lax.rem(loop + k, LOOP), thin), w_loop.at[k], 3 + k, ring[k - 1]))

    def w_third():
        for k in range(1, LOOP):
            w_copy(w_loop.at[k], w_loop.at[k], 3 + k, up).wait_recv()
        total = own_rows(w_z.at[0], loop, thin)[...]
        for k in range(1, LOOP):
            total += w_loop[k]
        w_pair[y * 2 + core] = total
        mine = w_pair.at[y * 2 + core]
        for k, where in ((0, sibling), (1, over), (2, diagonal)):
            go(w_copy(mine, mine, 11 + k, where))

    def w_fourth():
        for k, spot in ((0, y * 2 + 1 - core), (1, (1 - y) * 2 + core), (2, (1 - y) * 2 + 1 - core)):
            w_copy(w_pair.at[spot], w_pair.at[spot], 11 + k, up).wait_recv()
        total = ((w_pair[0] + w_pair[1]) + (w_pair[2] + w_pair[3])) * (1.0 / math.sqrt(ROWS * 128))
        mine = own_rows(w_all, loop, thin)
        mine[...] = total
        for k in range(1, LOOP):
            go(w_copy(mine, mine, 13 + k, ring[k - 1]))

    def w_fifth():
        for k in range(1, LOOP):
            theirs = own_rows(w_all, lax.rem(loop + LOOP - k, LOOP), thin)
            w_copy(theirs, theirs, 13 + k, up).wait_recv()
        mine = own_rows(wgrad, z, thick)
        mine[...] = w_all[...]
        for k, where in ((1, up), (2, far), (3, down)):
            go(w_copy(w_all, mine, 20 + k, where))

    def w_last():
        for k in range(1, Z):
            w_copy(w_all, own_rows(wgrad, zed(Z - k), thick), 20 + k, up).wait_recv()

    def multiply(f, start, end):
        def one(s, total):
            pair = jnp.concatenate([tiles[plan[0, 2 * s]], tiles[plan[0, 2 * s + 1]]], axis=0)
            source = jnp.concatenate([part[f][plan[1, 2 * s]], part[f][plan[1, 2 * s + 1]]], axis=1)
            term = jnp.dot(source, pair, preferred_element_type=F32)
            total = jnp.where(plan[2, s] != 0, total, 0.0) + term
            prefix[s] = total.astype(BF16)
            return total

        begin = jnp.zeros((HALF, TILE), F32) if start == 0 else acc[...]
        acc[...] = lax.fori_loop(start, end, one, begin, unroll=UNROLL)

    ys = (1 - y, y)
    order = [(2, 0), (1, 0), (3, 0), (2, 1), (0, 0), (1, 1), (3, 1), (0, 1)]

    def s_copy(f, k, i):
        return remote(sibbox.at[f, k, i], got.at[f, k, i], s_send.at[f, k, i], s_recv.at[f, k, i], sibling)

    def extract(f, box, k, i, cc):
        base = ((zed(k) * 2 + ys[i]) * 2 + cc) * BLOCKS

        def one(b, _):
            box[f, k, i, pl.ds(pl.multiple_of(b * TILE, TILE), TILE)] = prefix[plan[3, base + b]]
            return 0

        lax.fori_loop(0, BLOCKS, one, 0, unroll=BLOCKS)

    def split(f):
        for k, i in order:
            extract(f, sibbox, k, i, 1 - core)
            go(s_copy(f, k, i))

    taken = set()

    def take(f, k, i):
        if (f, k, i) not in taken:
            taken.add((f, k, i))
            extract(f, own, k, i, core)

    def take_all(f):
        for k, i in order:
            take(f, k, i)

    size = ROWS // 4
    ready = set()

    def chip(f, k, i, p, q):
        if (f, k, i) not in ready:
            ready.add((f, k, i))
            take(f, k, i)
            s_copy(f, k, i).wait_recv()
        rows = pl.ds((p * 2 + q) * size, size)
        return own[f, k, i, rows].astype(F32) + got[f, k, i, rows].astype(F32)

    def x_copy(f, k, p):
        return remote(xbox.at[f, k, p], xin.at[f, k, p], x_send.at[f, k, p], x_recv.at[f, k, p], over)

    def cross(f, k):
        for p in (0, 1):
            xbox[f, k, p] = chip(f, k, 0, p, 1).astype(BF16)
            go(x_copy(f, k, p))

    crossed = set()

    def term(f, k, u, p):
        if u < 2:
            return chip(f, k, u, p, 0)
        if (f, k, p) not in crossed:
            crossed.add((f, k, p))
            x_copy(f, k, p).wait_recv()
        return chip(f, k, 1, p, 1) + xin[f, k, p].astype(F32)

    def z_copy(f, kind, u, p, src, dst, where):
        return remote(src, dst, z_send.at[f, kind, u, p], z_recv.at[f, kind, u, p], where)

    ways = (up, down)
    near = (1, 3)

    def start_far(f, u):
        for p in (0, 1):
            box = outbox.at[f, 0, u, p]
            box[...] = term(f, 2, u, p).astype(BF16)
            go(z_copy(f, 0, u, p, box, relay_in.at[f, u, p], ways[p]))

    def start_plain(f, u):
        for p in (0, 1):
            box = outbox.at[f, 1, u, p]
            box[...] = term(f, near[p], u, 1 - p).astype(BF16)
            go(z_copy(f, 1, u, p, box, final_in.at[f, 0, u, 1 - p], ways[p]))

    def start_relayed(f, u):
        for p in (0, 1):
            z_copy(f, 0, u, p, relay_in.at[f, u, p], relay_in.at[f, u, p], up).wait_recv()
            box = outbox.at[f, 2, u, p]
            box[...] = (term(f, near[p], u, p) + relay_in[f, u, p].astype(F32)).astype(BF16)
            go(z_copy(f, 2, u, p, box, final_in.at[f, 1, u, p], ways[p]))

    def finish(f, u, p):
        z_copy(f, 1, u, 1 - p, final_in.at[f, 0, u, p], final_in.at[f, 0, u, p], up).wait_recv()
        z_copy(f, 2, u, p, final_in.at[f, 1, u, p], final_in.at[f, 1, u, p], up).wait_recv()
        return term(f, 0, u, p) + final_in[f, 0, u, p].astype(F32) + final_in[f, 1, u, p].astype(F32)

    def y_copy(f, p):
        return remote(ybox.at[f, p], yin.at[f, p], y_send.at[f, p], y_recv.at[f, p], over)

    def start_y(f):
        for p in (0, 1):
            ybox[f, p] = finish(f, 0, p).astype(BF16)
            go(y_copy(f, p))

    def write(f, p, q, total):
        for b in range(2):
            place = pl.ds(((p * 2 + q) * 2 + b) * TILE, TILE)
            node[place, f * HALF:(f + 1) * HALF] = total[b * TILE:(b + 1) * TILE].T

    def end_first(f):
        for p in (0, 1):
            total = finish(f, 1, p)
            y_copy(f, p).wait_recv()
            write(f, p, 0, total + yin[f, p].astype(F32))

    def end_second(f):
        for p in (0, 1):
            write(f, p, 1, finish(f, 2, p))

    cut = [0, STEPS // 2, STEPS]
    project(0)
    pl.semaphore_wait(barrier, arrivals)
    gather_own(0)
    project(1)
    for c in range(CHUNKS):
        w_term(c)
        gather_on(0, [c])
    w_first()
    gather_last(0)
    gather_own(1)
    gather_end(0)
    load.wait()
    multiply(0, cut[0], cut[1])
    w_second()
    gather_on(1, range(CHUNKS))
    multiply(0, cut[1], cut[2])
    split(0)
    w_third()
    gather_last(1)
    cross(0, 2)
    start_far(0, 0)
    start_plain(0, 0)
    cross(0, 1)
    cross(0, 3)
    start_far(0, 1)
    start_relayed(0, 0)
    start_plain(0, 1)
    cross(0, 0)
    start_far(0, 2)
    take_all(0)
    gather_end(1)
    w_fourth()
    multiply(1, cut[0], cut[1])
    start_relayed(0, 1)
    start_plain(0, 2)
    start_y(0)
    start_relayed(0, 2)
    w_fifth()
    multiply(1, cut[1], cut[2])
    split(1)
    cross(1, 2)
    start_far(1, 0)
    start_plain(1, 0)
    cross(1, 1)
    cross(1, 3)
    start_far(1, 1)
    end_first(0)
    start_relayed(1, 0)
    start_plain(1, 1)
    cross(1, 0)
    start_far(1, 2)
    start_relayed(1, 1)
    start_plain(1, 2)
    end_second(0)
    start_y(1)
    start_relayed(1, 2)
    end_first(1)
    end_second(1)
    w_last()
    for op in sent:
        op.wait_send()


def copy_kernel(node, wgrad, node_out, wgrad_out):
    node_out[...] = node[...]
    wgrad_out[...] = wgrad[...]


def shards(cotangent, preact, aggregated, weight, tile_values, tile_rows, tile_cols, tile_counts):
    dma = pltpu.SemaphoreType.DMA
    SMEM = pl.BlockSpec(memory_space=pltpu.SMEM)
    plan = pl.pallas_call(
        plan_kernel,
        out_shape=jax.ShapeDtypeStruct((4, WIDE), jnp.int32),
        in_specs=[VMEM, VMEM, SMEM],
        out_specs=VMEM,
        name="plan",
    )(tile_rows, tile_cols, tile_counts)

    size = (ROWS // 4, HALF)
    thick, thin = F // Z, F // Z // LOOP
    node, wgrad = pl.pallas_call(
        layer_kernel,
        out_shape=(
            jax.ShapeDtypeStruct((ROWS, F), F32),
            jax.ShapeDtypeStruct((F, F), F32),
        ),
        in_specs=[SMEM] + [VMEM] * 4 + [ANY],
        out_specs=(VMEM, VMEM),
        scratch_shapes=[
            pltpu.VMEM((SLOTS + 1, TILE, TILE), BF16),
            pltpu.VMEM((LOOP * BLOCKS, TILE, HALF), BF16),
            pltpu.VMEM((LOOP * BLOCKS, TILE, HALF), BF16),
            pltpu.VMEM((ROWS, F), BF16),
            pltpu.VMEM((STEPS + 1, TILE, HALF), BF16),
            pltpu.VMEM((TILE, HALF), F32),
            pltpu.VMEM((2, Z, 2, ROWS, HALF), BF16),
            pltpu.VMEM((2, Z, 2, ROWS, HALF), BF16),
            pltpu.VMEM((2, Z, 2, ROWS, HALF), BF16),
            pltpu.VMEM((2, 3, 2) + size, BF16),
            pltpu.VMEM((2, 2, 3, 2) + size, BF16),
            pltpu.VMEM((2, 3, 3, 2) + size, BF16),
            pltpu.VMEM((2, 2) + size, BF16),
            pltpu.VMEM((2, 2) + size, BF16),
            pltpu.VMEM((2, Z, 2) + size, BF16),
            pltpu.VMEM((2, Z, 2) + size, BF16),
            pltpu.VMEM((F, F), F32),
            pltpu.VMEM((Z, thick, F), F32),
            pltpu.VMEM((LOOP, thin, F), F32),
            pltpu.VMEM((4, thin, F), F32),
            pltpu.VMEM((thick, F), F32),
            dma,
            dma((2, 7, CHUNKS)), dma((2, 7, CHUNKS)),
            dma((2, Z, 2)), dma((2, Z, 2)),
            dma((2, 3, 3, 2)), dma((2, 3, 3, 2)),
            dma((2, 2)), dma((2, 2)),
            dma((2, Z, 2)), dma((2, Z, 2)),
            dma((24,)), dma((24,)),
        ],
        compiler_params=pltpu.CompilerParams(
            vmem_limit_bytes=60 * 1024 * 1024, collective_id=0, has_side_effects=True
        ),
        name="layer",
    )(plan, cotangent, preact, aggregated, weight, tile_values)
    return pl.pallas_call(
        copy_kernel,
        out_shape=(
            jax.ShapeDtypeStruct((ROWS, F), F32),
            jax.ShapeDtypeStruct((F, F), F32),
        ),
        grid=(4,),
        in_specs=[pl.BlockSpec((ROWS // 4, F), lambda g: (g, 0)), pl.BlockSpec((F // 4, F), lambda g: (g, 0))],
        out_specs=(pl.BlockSpec((ROWS // 4, F), lambda g: (g, 0)), pl.BlockSpec((F // 4, F), lambda g: (g, 0))),
        name="copies",
    )(node, wgrad)


def solution(mesh):
    split = P(("dom", "loop"))
    return jax.shard_map(
        shards,
        mesh=mesh,
        in_specs=(split, split, split, P(), split, split, split, split),
        out_specs=(split, P()),
        check_vma=False,
    )
```

```python
import functools
import math

import jax
import jax.numpy as jnp
from jax import lax
from jax.experimental import pallas as pl
from jax.experimental.pallas import tpu as pltpu
from jax.sharding import PartitionSpec as P

MESH = pl.DeviceIdType.MESH
VMEM = pl.BlockSpec(memory_space=pltpu.VMEM)
ANY = pl.BlockSpec(memory_space=pl.ANY)
F32 = jnp.float32
BF16 = jnp.bfloat16

ROWS = 1024
F = 256
TILE = 128
BLOCKS = 8
X = 4
LOOP = 8
Z = 4
HALF = F // 2
CHUNKS = 4
SLOTS = 640
STEPS = (SLOTS + 64) // 2
WIDE = 768
UNROLL = 88
CROSS = ((1, 2), (1,))


def remote(src, dst, send, recv, where):
    return pltpu.make_async_remote_copy(
        src_ref=src, dst_ref=dst, send_sem=send, recv_sem=recv, device_id=where, device_id_type=MESH
    )


def greet(peers):
    barrier = pltpu.get_barrier_semaphore()
    for peer in peers:
        pl.semaphore_signal(barrier, inc=1, device_id=peer, device_id_type=MESH)
    return barrier, len(peers)


def plan_kernel(rows, cols, count, out):
    blocks = 128

    def iota(shape, axis):
        return lax.broadcasted_iota(jnp.int32, shape, axis)

    def pick(mask, value, axis):
        return jnp.sum(jnp.where(mask, value, 0.0), axis=axis, keepdims=True)

    live = iota((1, SLOTS), 1) < count[0]
    hit = (iota((blocks, SLOTS), 0) == cols[...]) & live
    hits = jnp.where(hit, 1.0, 0.0)
    number = jnp.sum(hits, axis=1, keepdims=True)
    steps = jnp.floor((number + 1.0) * 0.5)
    down, along = iota((blocks, blocks), 0), iota((blocks, blocks), 1)
    steps_row = pick(down == along, steps, 0)
    first = pick(along < down, steps_row, 1)
    first_row = pick(down < along, steps, 0)
    out[3:4, 0:blocks] = jnp.where(steps_row > 0, first_row + steps_row - 1.0, float(STEPS)).astype(jnp.int32)
    out[3:4, blocks:] = jnp.zeros((1, WIDE - blocks), jnp.int32)

    big = (SLOTS, SLOTS)
    earlier = jnp.where(iota(big, 0) < iota(big, 1), 1.0, 0.0).astype(BF16)
    rank = jnp.dot(hits.astype(BF16), earlier, preferred_element_type=F32)
    place = jnp.where(live, pick(hit, 2.0 * first + rank, 0), 1000.0)
    both = place * 64.0 + rows[...].astype(F32)
    both = pick(iota(big, 0) == iota(big, 1), both, 1)
    place = jnp.floor(both * (1.0 / 64.0))
    row = both - place * 64.0
    found = place.astype(jnp.int32) == iota((SLOTS, WIDE), 1)
    tile = pick(found, iota((SLOTS, WIDE), 0).astype(F32) - float(SLOTS), 0) + float(SLOTS)
    out[0:1] = tile.astype(jnp.int32)
    out[1:2] = pick(found, row, 0).astype(jnp.int32)
    opens = (first.astype(jnp.int32) == iota((blocks, WIDE), 1)) & (steps > 0)
    out[2:3] = (1.0 - jnp.max(jnp.where(opens, 1.0, 0.0), axis=0, keepdims=True)).astype(jnp.int32)


def layer_kernel(
    plan, cot_hbm, pre_hbm, agg_hbm, w_hbm, tiles_hbm, node, wgrad,
    cot, pre, agg, w, tiles, part_a, part_b, masked, prefix, acc, own, sibbox, got, relay_in, final_in, outbox, ybox, yin, xbox, xin,
    wpart, w_parts, w_z, w_loop, w_pair, w_all,
    in_sem, tile_sem, g_send, g_recv, s_send, s_recv, z_send, z_recv, y_send, y_recv, x_send, x_recv, w_send, w_recv,
):
    dom, loop = lax.axis_index("dom"), lax.axis_index("loop")
    z, y, core = dom // 4, lax.rem(dom // 2, 2), lax.rem(dom, 2)
    x, high = lax.rem(loop, X), loop // X

    def at(zz, yy, cc):
        return {"dom": zz * 4 + yy * 2 + cc}

    def zed(k):
        return lax.rem(z + k, Z)

    sibling = at(z, y, 1 - core)
    up, far, down = at(zed(1), y, core), at(zed(2), y, core), at(zed(3), y, core)
    over = at(z, 1 - y, core)
    diagonal = at(z, 1 - y, 1 - core)
    right = {"loop": high * X + lax.rem(x + 1, X)}
    left = {"loop": high * X + lax.rem(x + X - 1, X)}
    across = {"loop": (1 - high) * X + x}
    ring = [{"loop": lax.rem(loop + k, LOOP)} for k in range(1, LOOP)]
    inputs = [
        pltpu.make_async_copy(source, target, in_sem.at[n])
        for n, (source, target) in enumerate(((pre_hbm, pre), (cot_hbm, cot), (w_hbm, w), (agg_hbm, agg)))
    ]
    for op in inputs:
        op.start()
    barrier, arrivals = greet([sibling, up, far, down, over, diagonal] + ring)

    load = pltpu.make_async_copy(tiles_hbm, tiles.at[pl.ds(0, SLOTS)], tile_sem)
    tiles[SLOTS] = jnp.zeros((TILE, TILE), BF16)
    prefix[STEPS] = jnp.zeros((TILE, HALF), BF16)
    sent = []

    def go(op):
        op.start()
        sent.append(op)

    part = (part_a, part_b)

    count = BLOCKS // CHUNKS

    def piece(f, hh, step, c):
        return part[f].at[pl.ds((hh * X + lax.rem(x + step, X)) * BLOCKS + c * count, count)]

    def g_copy(f, kind, c, ref, where):
        return remote(ref, ref, g_send.at[f, kind, c], g_recv.at[f, kind, c], where)

    def arrive(f, kind, c, ref):
        g_copy(f, kind, c, ref, right).wait_recv()

    back = [CHUNKS - 1 - c for c in range(CHUNKS)]

    def project(f):
        for c in range(2):
            rows = pl.ds(c * (ROWS // 2), ROWS // 2)
            if f == 0:
                masked[rows] = jnp.where(pre[rows].astype(F32) > 0, cot[rows].astype(F32), 0.0).astype(BF16)
            out = lax.dot_general(
                w[f * HALF:(f + 1) * HALF], masked[rows], (((1,), (1,)), ((), ())), preferred_element_type=F32
            ).astype(BF16)
            for b in range(BLOCKS // 2):
                part[f][loop * BLOCKS + c * (BLOCKS // 2) + b] = out[:, b * TILE:(b + 1) * TILE]

    def gather_own(f):
        for c, b, a in zip(range(CHUNKS), back, crossing(f)):
            go(g_copy(f, 0, c, piece(f, high, 0, c), right))
            go(g_copy(f, 1, b, piece(f, high, 0, b), left))
            go(g_copy(f, 2, a, piece(f, high, 0, a), across))

    def crossing(f):
        return sorted(range(CHUNKS), key=lambda c: c in CROSS[f])

    def gather_on(f, turns):
        for n in turns:
            c, b, a = n, back[n], crossing(f)[n]
            arrive(f, 0, c, piece(f, high, 3, c))
            if c < CHUNKS // 2:
                go(g_copy(f, 3, c, piece(f, high, 3, c), right))
            if c in CROSS[f]:
                go(g_copy(f, 4, c, piece(f, high, 3, c), across))
            arrive(f, 1, b, piece(f, high, 1, b))
            if b >= CHUNKS // 2:
                go(g_copy(f, 3, b, piece(f, high, 1, b), left))
            if b in CROSS[f]:
                go(g_copy(f, 5, b, piece(f, high, 1, b), across))
            arrive(f, 2, a, piece(f, 1 - high, 0, a))
            if a not in CROSS[f]:
                go(g_copy(f, 4, a, piece(f, 1 - high, 0, a), right))
                go(g_copy(f, 5, a, piece(f, 1 - high, 0, a), left))

    def gather_last(f):
        for c in CROSS[f]:
            arrive(f, 3, c, piece(f, high, 2, c))
            go(g_copy(f, 6, c, piece(f, high, 2, c), across))
        for c in range(CHUNKS):
            if c in CROSS[f]:
                continue
            arrive(f, 4, c, piece(f, 1 - high, 3, c))
            if c < CHUNKS // 2:
                go(g_copy(f, 6, c, piece(f, 1 - high, 3, c), right))
            arrive(f, 5, c, piece(f, 1 - high, 1, c))
            if c >= CHUNKS // 2:
                go(g_copy(f, 6, c, piece(f, 1 - high, 1, c), left))

    def gather_end(f):
        for c in range(CHUNKS):
            if c in CROSS[f]:
                arrive(f, 4, c, piece(f, 1 - high, 3, c))
                arrive(f, 5, c, piece(f, 1 - high, 1, c))
            else:
                arrive(f, 3, c, piece(f, high, 2, c))
            arrive(f, 6, c, piece(f, 1 - high, 2, c))

    thin = F // Z // LOOP

    def w_copy(src, dst, s, where):
        return remote(src, dst, w_send.at[s], w_recv.at[s], where)

    def own_rows(ref, index, size):
        return ref.at[pl.ds(pl.multiple_of(index * size, size), size)]

    def w_term(c):
        rows = pl.ds(c * (ROWS // 4), ROWS // 4)
        term = lax.dot_general(
            agg[rows], masked[rows], (((0,), (0,)), ((), ())), preferred_element_type=F32
        )
        wpart[...] = term if c == 0 else wpart[...] + term

    def w_first():
        for k in range(Z):
            for n in range(LOOP):
                w_parts[k, n * thin:(n + 1) * thin] = wpart[(n * Z + k) * thin:(n * Z + k + 1) * thin]
        for k, where in ((1, up), (2, far), (3, down)):
            go(w_copy(w_parts.at[zed(k)], w_z.at[k], k, where))

    def w_second():
        for k in range(1, Z):
            w_copy(w_z.at[k], w_z.at[k], k, up).wait_recv()
        total = w_parts[z]
        for k in range(1, Z):
            total += w_z[k]
        w_z[0] = total
        for k in range(1, LOOP):
            go(w_copy(own_rows(w_z.at[0], lax.rem(loop + k, LOOP), thin), w_loop.at[k], 3 + k, ring[k - 1]))

    def w_third():
        for k in range(1, LOOP):
            w_copy(w_loop.at[k], w_loop.at[k], 3 + k, up).wait_recv()
        total = own_rows(w_z.at[0], loop, thin)[...]
        for k in range(1, LOOP):
            total += w_loop[k]
        w_pair[y * 2 + core] = total
        mine = w_pair.at[y * 2 + core]
        for k, where in ((0, sibling), (1, over), (2, diagonal)):
            go(w_copy(mine, mine, 11 + k, where))

    def w_fourth():
        for k, spot in ((0, y * 2 + 1 - core), (1, (1 - y) * 2 + core), (2, (1 - y) * 2 + 1 - core)):
            w_copy(w_pair.at[spot], w_pair.at[spot], 11 + k, up).wait_recv()
        total = ((w_pair[0] + w_pair[1]) + (w_pair[2] + w_pair[3])) * (1.0 / math.sqrt(ROWS * 128))
        mine = own_rows(w_all, z, thin)
        mine[...] = total
        for k, where in ((1, up), (2, far), (3, down)):
            go(w_copy(mine, mine, 13 + k, where))

    def w_fifth():
        for k in range(1, Z):
            theirs = own_rows(w_all, zed(Z - k), thin)
            w_copy(theirs, theirs, 13 + k, up).wait_recv()
        mine = own_rows(wgrad, loop, thin * Z)
        mine[...] = w_all[...]
        for k in range(1, LOOP):
            go(w_copy(w_all, mine, 16 + k, ring[k - 1]))

    def w_last():
        for k in range(1, LOOP):
            theirs = own_rows(wgrad, lax.rem(loop + LOOP - k, LOOP), thin * Z)
            w_copy(w_all, theirs, 16 + k, up).wait_recv()

    def multiply(f, start, end):
        def one(s, total):
            pair = jnp.concatenate([tiles[plan[0, 2 * s]], tiles[plan[0, 2 * s + 1]]], axis=0)
            source = jnp.concatenate([part[f][plan[1, 2 * s]], part[f][plan[1, 2 * s + 1]]], axis=1)
            term = jnp.dot(source, pair, preferred_element_type=F32)
            total = jnp.where(plan[2, s] != 0, total, 0.0) + term
            prefix[s] = total.astype(BF16)
            return total

        begin = jnp.zeros((HALF, TILE), F32) if start == 0 else acc[...]
        acc[...] = lax.fori_loop(start, end, one, begin, unroll=UNROLL)

    ys = (1 - y, y)
    order = [(2, 0), (1, 0), (3, 0), (2, 1), (0, 0), (1, 1), (3, 1), (0, 1)]

    def s_copy(f, k, i):
        return remote(sibbox.at[f, k, i], got.at[f, k, i], s_send.at[f, k, i], s_recv.at[f, k, i], sibling)

    def extract(f, box, k, i, cc):
        base = ((zed(k) * 2 + ys[i]) * 2 + cc) * BLOCKS

        def one(b, _):
            box[f, k, i, pl.ds(pl.multiple_of(b * TILE, TILE), TILE)] = prefix[plan[3, base + b]]
            return 0

        lax.fori_loop(0, BLOCKS, one, 0, unroll=BLOCKS)

    def split(f):
        for k, i in order:
            extract(f, sibbox, k, i, 1 - core)
            go(s_copy(f, k, i))

    taken = set()

    def take(f, k, i):
        if (f, k, i) not in taken:
            taken.add((f, k, i))
            extract(f, own, k, i, core)

    def take_all(f):
        for k, i in order:
            take(f, k, i)

    size = ROWS // 4
    ready = set()

    def chip(f, k, i, p, q):
        if (f, k, i) not in ready:
            ready.add((f, k, i))
            take(f, k, i)
            s_copy(f, k, i).wait_recv()
        rows = pl.ds((p * 2 + q) * size, size)
        return own[f, k, i, rows].astype(F32) + got[f, k, i, rows].astype(F32)

    def x_copy(f, k, p):
        return remote(xbox.at[f, k, p], xin.at[f, k, p], x_send.at[f, k, p], x_recv.at[f, k, p], over)

    def cross(f, k):
        for p in (0, 1):
            xbox[f, k, p] = chip(f, k, 0, p, 1).astype(BF16)
            go(x_copy(f, k, p))

    crossed = set()

    def term(f, k, u, p):
        if u < 2:
            return chip(f, k, u, p, 0)
        if (f, k, p) not in crossed:
            crossed.add((f, k, p))
            x_copy(f, k, p).wait_recv()
        return chip(f, k, 1, p, 1) + xin[f, k, p].astype(F32)

    def z_copy(f, kind, u, p, src, dst, where):
        return remote(src, dst, z_send.at[f, kind, u, p], z_recv.at[f, kind, u, p], where)

    ways = (up, down)
    near = (1, 3)

    def start_far(f, u):
        for p in (0, 1):
            box = outbox.at[f, 0, u, p]
            box[...] = term(f, 2, u, p).astype(BF16)
            go(z_copy(f, 0, u, p, box, relay_in.at[f, u, p], ways[p]))

    def start_plain(f, u):
        for p in (0, 1):
            box = outbox.at[f, 1, u, p]
            box[...] = term(f, near[p], u, 1 - p).astype(BF16)
            go(z_copy(f, 1, u, p, box, final_in.at[f, 0, u, 1 - p], ways[p]))

    def start_relayed(f, u):
        for p in (0, 1):
            z_copy(f, 0, u, p, relay_in.at[f, u, p], relay_in.at[f, u, p], up).wait_recv()
            box = outbox.at[f, 2, u, p]
            box[...] = (term(f, near[p], u, p) + relay_in[f, u, p].astype(F32)).astype(BF16)
            go(z_copy(f, 2, u, p, box, final_in.at[f, 1, u, p], ways[p]))

    def finish(f, u, p):
        z_copy(f, 1, u, 1 - p, final_in.at[f, 0, u, p], final_in.at[f, 0, u, p], up).wait_recv()
        z_copy(f, 2, u, p, final_in.at[f, 1, u, p], final_in.at[f, 1, u, p], up).wait_recv()
        return term(f, 0, u, p) + final_in[f, 0, u, p].astype(F32) + final_in[f, 1, u, p].astype(F32)

    def y_copy(f, p):
        return remote(ybox.at[f, p], yin.at[f, p], y_send.at[f, p], y_recv.at[f, p], over)

    def start_y(f):
        for p in (0, 1):
            ybox[f, p] = finish(f, 0, p).astype(BF16)
            go(y_copy(f, p))

    def write(f, p, q, total):
        for b in range(2):
            place = pl.ds(((p * 2 + q) * 2 + b) * TILE, TILE)
            node[place, f * HALF:(f + 1) * HALF] = total[b * TILE:(b + 1) * TILE].T

    def end_first(f):
        for p in (0, 1):
            total = finish(f, 1, p)
            y_copy(f, p).wait_recv()
            write(f, p, 0, total + yin[f, p].astype(F32))

    def end_second(f):
        for p in (0, 1):
            write(f, p, 1, finish(f, 2, p))

    cut = [0, 88, 176, 264, STEPS]
    for op in inputs:
        op.wait()
    load.start()
    project(0)
    pl.semaphore_wait(barrier, arrivals)
    gather_own(0)
    project(1)
    for c in range(CHUNKS):
        w_term(c)
        gather_on(0, [c])
    w_first()
    gather_last(0)
    gather_own(1)
    gather_end(0)
    load.wait()
    multiply(0, cut[0], cut[1])
    w_second()
    multiply(0, cut[1], cut[2])
    gather_on(1, [0, 1])
    multiply(0, cut[2], cut[3])
    gather_on(1, [2, 3])
    multiply(0, cut[3], cut[4])
    split(0)
    w_third()
    gather_last(1)
    cross(0, 2)
    start_far(0, 0)
    start_plain(0, 0)
    cross(0, 1)
    cross(0, 3)
    start_far(0, 1)
    start_relayed(0, 0)
    start_plain(0, 1)
    cross(0, 0)
    start_far(0, 2)
    take_all(0)
    gather_end(1)
    w_fourth()
    multiply(1, cut[0], cut[1])
    start_relayed(0, 1)
    start_plain(0, 2)
    multiply(1, cut[1], cut[2])
    start_relayed(0, 2)
    multiply(1, cut[2], cut[3])
    start_y(0)
    w_fifth()
    multiply(1, cut[3], cut[4])
    split(1)
    cross(1, 2)
    start_far(1, 0)
    start_plain(1, 0)
    cross(1, 1)
    cross(1, 3)
    start_far(1, 1)
    end_first(0)
    start_relayed(1, 0)
    start_plain(1, 1)
    cross(1, 0)
    start_far(1, 2)
    start_relayed(1, 1)
    start_plain(1, 2)
    end_second(0)
    start_y(1)
    start_relayed(1, 2)
    end_first(1)
    end_second(1)
    w_last()
    for op in sent:
        op.wait_send()


def copy_kernel(node, wgrad, node_out, wgrad_out):
    node_out[...] = node[...]
    wgrad_out[...] = wgrad[...]


def shards(cotangent, preact, aggregated, weight, tile_values, tile_rows, tile_cols, tile_counts):
    dma = pltpu.SemaphoreType.DMA
    SMEM = pl.BlockSpec(memory_space=pltpu.SMEM)
    plan = pl.pallas_call(
        plan_kernel,
        out_shape=jax.ShapeDtypeStruct((4, WIDE), jnp.int32),
        in_specs=[VMEM, VMEM, SMEM],
        out_specs=VMEM,
        name="plan",
    )(tile_rows, tile_cols, tile_counts)

    size = (ROWS // 4, HALF)
    thick, thin = F // Z, F // Z // LOOP
    node, wgrad = pl.pallas_call(
        layer_kernel,
        out_shape=(
            jax.ShapeDtypeStruct((ROWS, F), F32),
            jax.ShapeDtypeStruct((F, F), F32),
        ),
        in_specs=[SMEM] + [ANY] * 5,
        out_specs=(VMEM, VMEM),
        scratch_shapes=[
            pltpu.VMEM((ROWS, F), BF16),
            pltpu.VMEM((ROWS, F), BF16),
            pltpu.VMEM((ROWS, F), BF16),
            pltpu.VMEM((F, F), BF16),
            pltpu.VMEM((SLOTS + 1, TILE, TILE), BF16),
            pltpu.VMEM((LOOP * BLOCKS, TILE, HALF), BF16),
            pltpu.VMEM((LOOP * BLOCKS, TILE, HALF), BF16),
            pltpu.VMEM((ROWS, F), BF16),
            pltpu.VMEM((STEPS + 1, TILE, HALF), BF16),
            pltpu.VMEM((TILE, HALF), F32),
            pltpu.VMEM((2, Z, 2, ROWS, HALF), BF16),
            pltpu.VMEM((2, Z, 2, ROWS, HALF), BF16),
            pltpu.VMEM((2, Z, 2, ROWS, HALF), BF16),
            pltpu.VMEM((2, 3, 2) + size, BF16),
            pltpu.VMEM((2, 2, 3, 2) + size, BF16),
            pltpu.VMEM((2, 3, 3, 2) + size, BF16),
            pltpu.VMEM((2, 2) + size, BF16),
            pltpu.VMEM((2, 2) + size, BF16),
            pltpu.VMEM((2, Z, 2) + size, BF16),
            pltpu.VMEM((2, Z, 2) + size, BF16),
            pltpu.VMEM((F, F), F32),
            pltpu.VMEM((Z, thick, F), F32),
            pltpu.VMEM((Z, thick, F), F32),
            pltpu.VMEM((LOOP, thin, F), F32),
            pltpu.VMEM((4, thin, F), F32),
            pltpu.VMEM((Z * thin, F), F32),
            dma((4,)), dma,
            dma((2, 7, CHUNKS)), dma((2, 7, CHUNKS)),
            dma((2, Z, 2)), dma((2, Z, 2)),
            dma((2, 3, 3, 2)), dma((2, 3, 3, 2)),
            dma((2, 2)), dma((2, 2)),
            dma((2, Z, 2)), dma((2, Z, 2)),
            dma((24,)), dma((24,)),
        ],
        compiler_params=pltpu.CompilerParams(
            vmem_limit_bytes=60 * 1024 * 1024, collective_id=0, has_side_effects=True
        ),
        name="layer",
    )(plan, cotangent, preact, aggregated, weight, tile_values)
    return pl.pallas_call(
        copy_kernel,
        out_shape=(
            jax.ShapeDtypeStruct((ROWS, F), F32),
            jax.ShapeDtypeStruct((F, F), F32),
        ),
        in_specs=[VMEM, VMEM],
        out_specs=(VMEM, VMEM),
        name="copies",
    )(node, wgrad)


def solution(mesh):
    split = P(("dom", "loop"))
    return jax.shard_map(
        shards,
        mesh=mesh,
        in_specs=(split, split, split, P(), split, split, split, split),
        out_specs=(split, P()),
        check_vma=False,
    )
```
